256 devices in a mesh: ctx: 32 (over x, y, core), head: 8 (over z).
Axes of the slice: x: 4, y: 4, z: 8, core: 2. Of those that a mesh axis runs over, the one named last changes fastest.
Arguments:
- query: bfloat16 [512, 64, 128], P('ctx', 'head'), may hold values from -6 to 6
- weights: bfloat16 [512, 64], P('ctx', 'head'), as said below
- keys: bfloat16 [65536, 128], P('ctx'), may hold values from -6 to 6
- main_logits: bfloat16 [512, 65536], P(None, 'ctx'), as said below
- row_weight: float32 [512], replicated, may hold values from 4 to 40
- offset: int32 [1], replicated, may hold values from 64512 to 65024
Outputs:
- query_grad: float32 [512, 64, 128], P('ctx', 'head')
- key_grad: float32 [65536, 128], P(('ctx', 'head'))
- weight_grad: float32 [512, 64], P('ctx', 'head')
The draws below stay inside these ranges and needn't reach their ends.
Inputs may be any that keep to these rules, and one draw needn't show every extreme that they name: query row t of the block sits at position offset + t. Finite weights. `main_logits`: finite logits.
All inputs are finite; a program needn't handle non-finite values.
Results may differ from the reference program's by a relative error of at most 0.0065.
Values may be sent and summed in bfloat16 or wider, within the bound.
A program may use at most 64 MiB of HBM per device.

```python
import math
import jax
import jax.numpy as jnp
from jax import lax

H = 64
DH = 128
Q_ROWS = 512
KEYS = 65536


def draw_weights(key, part):
    key = jax.random.fold_in(key, 11)
    values = jnp.clip(jax.random.normal(jax.random.fold_in(key, 1), (Q_ROWS, H), jnp.float32), -6.0, 6.0) * H ** (-0.5)
    return values.astype(jnp.bfloat16)


def draw_main_logits(key, part):
    key = jax.random.fold_in(key, 12)
    values = 1.5 * jnp.clip(jax.random.normal(jax.random.fold_in(key, 1), (Q_ROWS, KEYS), jnp.float32), -6.0, 6.0)
    return values.astype(jnp.bfloat16)


def block_levels(key, dims, split, low, top_value):
    def one(axis_at, blocks):
        draws = jax.random.uniform(jax.random.fold_in(jax.random.fold_in(key, 6), axis_at), (blocks,), jnp.float32, low / len(split), top_value / len(split))
        return jnp.repeat(jnp.exp(draws), dims[axis_at] // blocks).reshape((-1,) + (1,) * (len(dims) - axis_at - 1))

    gain = one(*split[0])
    for cut in split[1:]:
        gain = gain * one(*cut)
    return gain


def noise(key, extent, scale, reach, pieces=(), held_as=jnp.bfloat16):
    entries = jax.random.normal(key, extent, jnp.float32) * scale
    if len(pieces) > 0:
        entries = block_levels(key, extent, pieces, -0.22, 0.18) * entries
    return jnp.clip(entries, min=-reach, max=reach).astype(held_as)


def setup_inputs(seed: int = 0) -> dict:
    splits = jax.random.split(jax.random.key(seed), 7)
    return {
        "query": noise(splits[0], (Q_ROWS, H, DH), 1.0, 6.0, ((0, 32), (1, 8))),
        "weights": draw_weights(jax.random.fold_in(splits[6], 71), 0),
        "keys": noise(splits[2], (KEYS, DH), 1.0, 6.0, ((0, 32),)),
        "main_logits": draw_main_logits(jax.random.fold_in(splits[6], 71), 0),
        "row_weight": jnp.clip(jnp.exp(jax.random.uniform(splits[4], (Q_ROWS,), jnp.float32, math.log(4.0), math.log(40.0))), 4.0, 40.0),
        "offset": jax.random.randint(splits[5], (1,), KEYS - 2 * Q_ROWS, KEYS - Q_ROWS + 1).astype(jnp.int32),
    }


masked_value = -1e30


def softmax_rows(values, allowed):
    masked = jnp.where(allowed, values, masked_value)
    peak = jnp.max(masked, axis=1, keepdims=True)
    expd = jnp.where(allowed, jnp.exp(masked - peak), 0.0)
    return expd / jnp.sum(expd, axis=1, keepdims=True)


def reference(query, weights, keys, main_logits, row_weight, offset):
    head_scale = DH ** -0.5
    loss_scale = KEYS ** 0.5
    block_len = min(1024, KEYS)
    nblocks = KEYS // block_len
    query_f = query.astype(jnp.float32)
    weight_f = weights.astype(jnp.float32)
    key_blocks = keys.reshape(nblocks, block_len, DH)
    high = lax.Precision.HIGHEST

    def forward_block(key_block):
        dotted = jnp.einsum('thd,sd->ths', query_f, key_block.astype(jnp.float32), precision=high)
        active = jnp.maximum(dotted, 0.0) * head_scale
        return jnp.einsum('th,ths->ts', weight_f, active, precision=high)

    score = jnp.moveaxis(lax.map(forward_block, key_blocks), 0, 1).reshape(Q_ROWS, KEYS)
    row_ids = jnp.arange(Q_ROWS, dtype=jnp.int32)[:, None]
    columns = jnp.arange(KEYS, dtype=jnp.int32)[None, :]
    allowed = columns <= offset[0] + row_ids
    index_prob = softmax_rows(score, allowed)
    target = softmax_rows(main_logits.astype(jnp.float32), allowed)
    score_grad = jnp.where(allowed, row_weight[:, None] * loss_scale * (index_prob - target), 0.0).astype(jnp.bfloat16)
    grad_blocks = jnp.moveaxis(score_grad.reshape(Q_ROWS, nblocks, block_len), 1, 0)

    def backward_block(carry, inputs):
        query_acc, weight_acc = carry
        key_block, grad_block = inputs
        key_f = key_block.astype(jnp.float32)
        dotted = jnp.einsum('thd,sd->ths', query_f, key_f, precision=high)
        active = jnp.maximum(dotted, 0.0) * head_scale
        grad_f = grad_block.astype(jnp.float32)
        pre_grad = jnp.where(dotted > 0, grad_f[:, None, :] * weight_f[:, :, None] * head_scale, 0.0)
        pre_grad = pre_grad.astype(jnp.bfloat16).astype(jnp.float32)
        query_acc = query_acc + jnp.einsum('ths,sd->thd', pre_grad, key_f, precision=high)
        weight_acc = weight_acc + jnp.einsum('ts,ths->th', grad_f, active, precision=high)
        key_part = jnp.einsum('ths,thd->sd', pre_grad, query_f, precision=high)
        return (query_acc, weight_acc), key_part

    start_carry = (jnp.zeros((Q_ROWS, H, DH), jnp.float32), jnp.zeros((Q_ROWS, H), jnp.float32))
    (query_grad, weight_grad), key_parts = lax.scan(backward_block, start_carry, (key_blocks, grad_blocks))
    return query_grad, key_parts.reshape(KEYS, DH), weight_grad
```

```python
import functools

import jax
import jax.numpy as jnp
from jax import lax
from jax.experimental import pallas as pl
from jax.experimental.pallas import tpu as pltpu
from jax.sharding import PartitionSpec as P

MESH = pl.DeviceIdType.MESH
masked_value = -1e30
bf16 = jnp.bfloat16
f32 = jnp.float32

NX, NY, NZ = 4, 4, 8
CHIPS = NX * NY
SLOTS = 2 * CHIPS
ROWS = 64
KEYS = 2048
DH = 128
BLOCK = 128
GROUP = 4
CHUNK = 256
NCHUNK = KEYS // CHUNK


def iota(shape, dim):
    return lax.broadcasted_iota(jnp.int32, shape, dim)


def fold_rows(tiles):
    sub = iota(tiles[0].shape, 0)
    for k in (4, 2, 1):
        low = (sub & k) == 0
        half = len(tiles) // 2
        out = []
        for a, b in zip(tiles[:half], tiles[half:]):
            out.append(
                jnp.where(low, a + pltpu.roll(a, 8 - k, 0), b + pltpu.roll(b, k, 0))
            )
        tiles = out
    return tiles[0]


def kernel(
    query,
    weights,
    keys_hbm,
    logits_hbm,
    row_weight,
    offset,
    query_grad,
    key_grad,
    weight_grad,
    keys,
    keys_t,
    logits,
    send_a,
    recv_a,
    slots,
    relu,
    score,
    target,
    grad_rows,
    query_w,
    row_scale,
    stat_own,
    stat_in,
    sib_out,
    sib_in,
    sum_out,
    sum_in,
    ring_out,
    ring_in,
    back_out,
    back_in,
    local_sem,
    a_send,
    a_recv,
    g_send,
    g_recv,
    s_send,
    s_recv,
    st_send,
    st_recv,
    sib_send,
    sib_recv,
    sum_send,
    sum_recv,
    ring_send,
    ring_recv,
    back_send,
    back_recv,
):
    ctx = lax.axis_index("ctx")
    z = lax.axis_index("head")
    core = ctx % 2
    chip = ctx // 2
    x = chip // NY
    y = chip % NY
    head_scale = DH**-0.5
    loss_scale = float(KEYS * 32) ** 0.5

    def chip_at(dx, dy):
        return ((x + dx) % NX) * NY + (y + dy) % NY

    def dev_chip(dx, dy):
        return {"ctx": chip_at(dx, dy) * 2 + core, "head": z}

    def dev_z(dz):
        return {"ctx": ctx, "head": (z + dz) % NZ}

    sibling = {"ctx": chip * 2 + (1 - core), "head": z}

    def send(src, dst, send_sem, recv_sem, device):
        copy = pltpu.make_async_remote_copy(
            src_ref=src,
            dst_ref=dst,
            send_sem=send_sem,
            recv_sem=recv_sem,
            device_id=device,
            device_id_type=MESH,
        )
        copy.start()
        return copy

    load_keys = pltpu.make_async_copy(keys_hbm, keys, local_sem.at[0])
    load_keys.start()
    load_logits = pltpu.make_async_copy(logits_hbm, logits, local_sem.at[1])
    load_logits.start()
    barrier = pltpu.get_barrier_semaphore()

    def greet(i, carry):
        pl.semaphore_signal(
            barrier, inc=1, device_id=dev_chip(i // NY, i % NY), device_id_type=MESH
        )
        return carry

    lax.fori_loop(1, CHIPS, greet, 0)

    def greet_z(i, carry):
        pl.semaphore_signal(barrier, inc=1, device_id=dev_z(i), device_id_type=MESH)
        return carry

    lax.fori_loop(1, NZ, greet_z, 0)
    pl.semaphore_signal(barrier, inc=1, device_id=sibling, device_id_type=MESH)

    w_own = weights[...].astype(f32)
    lane = iota((8, 128), 1)
    place = jnp.where(
        (lane % 8 == iota((8, 128), 0)) & ((lane % 64) // 8 == z), 1.0, 0.0
    ).astype(f32)
    w_spread = jnp.dot(w_own, place, preferred_element_type=f32)
    pair = iota((16, 128), 0) % 2 == iota((16, 128), 1) // 64
    w_spread = jnp.where(pair, w_spread, 0.0)
    for to in range(NZ):
        send_a[to, 0:16, :] = query[16 * to : 16 * to + 16, :]
        row = w_spread[2 * to : 2 * to + 1, :] + w_spread[2 * to + 1 : 2 * to + 2, :]
        send_a[to, 16:32, :] = jnp.broadcast_to(row, (16, 128)).astype(bf16)

    def row_of(shape):
        r = iota(shape, 0)
        slot = (r // 8) * 4 + r % 4
        return 16 * ((slot % CHIPS) * 2 + slot // CHIPS) + 2 * z + (r // 4) % 2

    here = row_of((ROWS, 512)) == iota((ROWS, 512), 1)
    rw_col = jnp.sum(jnp.where(here, row_weight[...], 0.0), axis=1, keepdims=True)
    row_scale[...] = jnp.broadcast_to(rw_col * loss_scale, (ROWS, 128))

    load_keys.wait()
    for i in range(KEYS // 256):
        keys_t[:, 256 * i : 256 * i + 256] = (
            keys[256 * i : 256 * i + 256, :].astype(f32).T.astype(bf16)
        )
    load_logits.wait()
    pick = jnp.where(here, 1.0, 0.0).astype(bf16)
    limit = offset[0] - ctx * KEYS
    allowed = iota((ROWS, KEYS), 1) <= limit + row_of((ROWS, KEYS))
    tmasked = jnp.where(
        allowed, jnp.dot(pick, logits[...], preferred_element_type=f32), masked_value
    )
    tpeak = jnp.max(tmasked, axis=1, keepdims=True)
    texp = jnp.where(allowed, jnp.exp(tmasked - tpeak), 0.0)
    target[...] = texp
    ttotal = jnp.sum(texp, axis=1, keepdims=True)

    pl.semaphore_wait(barrier, CHIPS - 1 + NZ - 1 + 1)

    def start_a(i, carry):
        to = (z + i) % NZ
        send(send_a.at[to], recv_a.at[z], a_send.at[i], a_recv.at[i], dev_z(i))
        return carry

    lax.fori_loop(1, NZ, start_a, 0)
    recv_a[pl.ds(z, 1)] = send_a[pl.ds(z, 1)]

    def wait_a(i, carry):
        pltpu.make_async_remote_copy(
            src_ref=send_a.at[(z + i) % NZ],
            dst_ref=recv_a.at[(z + NZ - i) % NZ],
            send_sem=a_send.at[i],
            recv_sem=a_recv.at[i],
            device_id=dev_z(i),
            device_id_type=MESH,
        ).wait()
        return carry

    lax.fori_loop(1, NZ, wait_a, 0)
    own_slot = core * CHIPS + chip
    got = recv_a[...].astype(f32)
    mine = got[:, 0:16, :].reshape(8, 2, 8, DH)
    own = jnp.concatenate([mine[:, 0].reshape(64, DH), mine[:, 1].reshape(64, DH)], axis=0)
    own_w = jnp.sum(got[:, 16:32, :], axis=0)
    slots[pl.ds(own_slot, 1), 0:BLOCK, :] = own.astype(bf16)[None]
    slots[pl.ds(own_slot, 1), BLOCK : BLOCK + 16, :] = own_w.astype(bf16)[None]

    def start_g(i, carry):
        send(
            slots.at[own_slot],
            slots.at[own_slot],
            g_send.at[i],
            g_recv.at[i],
            dev_chip(i // NY, i % NY),
        )
        return carry

    lax.fori_loop(1, CHIPS, start_g, 0)

    def relay(i, carry):
        slot = core * CHIPS + chip_at(NX - i // NY, NY - i % NY)

        @pl.when(i > 0)
        def _():
            pltpu.make_async_remote_copy(
                src_ref=slots.at[own_slot],
                dst_ref=slots.at[slot],
                send_sem=g_send.at[i],
                recv_sem=g_recv.at[i],
                device_id=dev_chip(i // NY, i % NY),
                device_id_type=MESH,
            ).wait()

        send(slots.at[slot], slots.at[slot], s_send.at[i], s_recv.at[i], sibling)
        return carry

    lax.fori_loop(0, CHIPS, relay, 0)

    def wait_relay(i, carry):
        p = chip_at(NX - i // NY, NY - i % NY)
        pltpu.make_async_remote_copy(
            src_ref=slots.at[core * CHIPS + p],
            dst_ref=slots.at[(1 - core) * CHIPS + p],
            send_sem=s_send.at[i],
            recv_sem=s_recv.at[i],
            device_id=sibling,
            device_id_type=MESH,
        ).wait()
        return carry

    lax.fori_loop(0, CHIPS, wait_relay, 0)

    def forward(gi, carry):
        block = slots[pl.ds(gi * GROUP, GROUP)]
        q = block[:, 0:BLOCK, :].reshape(GROUP * BLOCK, DH)
        w_tiles = []
        for i in range(GROUP):
            w_row = block[i, BLOCK : BLOCK + 16, :].astype(f32)[0:1] * head_scale
            w_col = jnp.broadcast_to(w_row, (128, 128)).T
            w_tiles.append(w_col.reshape(2, 8, 8, 128))
            qw = block[i, 0:BLOCK, :].astype(f32) * w_col
            query_w[:, pl.ds(pl.multiple_of((gi * GROUP + i) * 128, 128), 128)] = qw.T.astype(bf16)
        for c in range(NCHUNK):
            at = slice(c * CHUNK, (c + 1) * CHUNK)
            dotted = jnp.dot(q, keys_t[:, at], preferred_element_type=f32)
            active = jnp.maximum(dotted, 0.0)
            relu[pl.ds(gi * GROUP, GROUP), :, at] = active.reshape(GROUP, BLOCK, CHUNK).astype(bf16)
            active = active.reshape(GROUP, 2, 8, 8, CHUNK)
            for l in range(CHUNK // 128):
                tiles = []
                for j in range(2):
                    for i in range(GROUP):
                        part = active[i, j, :, :, l * 128 : l * 128 + 128] * w_tiles[i][j]
                        tiles.append(jnp.sum(part, axis=0))
                score[
                    pl.ds(pl.multiple_of(gi * 8, 8), 8),
                    c * CHUNK + l * 128 : c * CHUNK + l * 128 + 128,
                ] = fold_rows(tiles)
        return carry

    lax.fori_loop(0, SLOTS // GROUP, forward, 0)

    masked = jnp.where(allowed, score[...], masked_value)
    peak = jnp.max(masked, axis=1, keepdims=True)
    exps = jnp.where(allowed, jnp.exp(masked - peak), 0.0)
    score[...] = exps
    total = jnp.sum(exps, axis=1, keepdims=True)
    lane = iota((ROWS, 128), 1)
    stats = jnp.where(
        lane == 0,
        peak,
        jnp.where(lane == 1, total, jnp.where(lane == 2, tpeak, jnp.where(lane == 3, ttotal, 0.0))),
    )
    stats = jnp.concatenate([stats, jnp.zeros((128 - ROWS, 128), f32)], axis=0).T[0:8]
    local_stats = stats

    def merge(parts):
        rows = []
        for k in (0, 2):
            top = functools.reduce(jnp.maximum, [p[k : k + 1] for p in parts])
            rows.append(top)
            rows.append(sum(p[k + 1 : k + 2] * jnp.exp(p[k : k + 1] - top) for p in parts))
        return jnp.concatenate(rows + [jnp.zeros((4, 128), f32)], axis=0)

    at = 0
    for stage, peers in enumerate(
        (
            [sibling],
            [dev_chip(0, d) for d in (1, 2, 3)],
            [dev_chip(d, 0) for d in (1, 2, 3)],
        )
    ):
        stat_own[stage] = stats
        copies = []
        for n, peer in enumerate(peers):
            copies.append(
                send(
                    stat_own.at[stage],
                    stat_in.at[at + n],
                    st_send.at[at + n],
                    st_recv.at[at + n],
                    peer,
                )
            )
        for copy in copies:
            copy.wait()
        stats = merge([stats] + [stat_in[at + n] for n in range(len(peers))])
        at += len(peers)

    shares = [
        jnp.exp(local_stats[k : k + 1] - stats[k : k + 1]) / stats[k + 1 : k + 2] for k in (0, 2)
    ]
    shares = jnp.concatenate(shares + [jnp.zeros((126, 128), f32)], axis=0).T[0:ROWS]
    prob_scale = shares[:, 0:1] * row_scale[:, 0:1]
    target_scale = shares[:, 1:2] * row_scale[:, 0:1]
    score[...] = score[...] * prob_scale - target[...] * target_scale

    def backward_query(gi):
        tile = score[pl.ds(pl.multiple_of(gi * 8, 8), 8), :]
        acc = jnp.zeros((GROUP * BLOCK, DH), f32)
        for c in range(NCHUNK):
            at = slice(c * CHUNK, (c + 1) * CHUNK)
            parts = []
            for i in range(GROUP):
                for j in range(2):
                    row = tile[j * 4 + i : j * 4 + i + 1, at]
                    row = jnp.broadcast_to(row, (16, CHUNK)).astype(bf16)
                    grad_rows[gi * GROUP + i, j, :, at] = row
                    act = relu[gi * GROUP + i, j * 64 : j * 64 + 64, at].reshape(4, 16, CHUNK)
                    parts.append(jnp.where(act > 0, row[None], jnp.zeros_like(act)).reshape(64, CHUNK))
            pre = jnp.concatenate(parts, axis=0)
            acc = acc + jnp.dot(pre, keys[at, :], preferred_element_type=f32)
        return acc.reshape(GROUP, BLOCK, DH)

    def for_sibling(g, carry):
        acc = backward_query((1 - core) * (CHIPS // GROUP) + g)
        sib_out[pl.ds(g * GROUP, GROUP)] = acc.astype(bf16)
        send(
            sib_out.at[pl.ds(g * GROUP, GROUP)],
            sib_in.at[pl.ds(g * GROUP, GROUP)],
            sib_send.at[g],
            sib_recv.at[g],
            sibling,
        )
        return carry

    lax.fori_loop(0, CHIPS // GROUP, for_sibling, 0)

    def for_chips(n, carry):
        dx = (n + 2) % NX
        g = (x + dx) % NX
        acc = backward_query(core * (CHIPS // GROUP) + g)
        pltpu.make_async_remote_copy(
            src_ref=sib_out.at[pl.ds(g * GROUP, GROUP)],
            dst_ref=sib_in.at[pl.ds(g * GROUP, GROUP)],
            send_sem=sib_send.at[g],
            recv_sem=sib_recv.at[g],
            device_id=sibling,
            device_id_type=MESH,
        ).wait()
        acc = acc + sib_in[pl.ds(g * GROUP, GROUP)].astype(f32)
        sum_out[pl.ds(g * GROUP, GROUP)] = acc.astype(bf16)

        def to_chip(dy, c2):
            i = dx * NY + dy

            @pl.when(i > 0)
            def _():
                send(
                    sum_out.at[chip_at(dx, dy)],
                    sum_in.at[i],
                    sum_send.at[i],
                    sum_recv.at[i],
                    dev_chip(dx, dy),
                )

            return c2

        lax.fori_loop(0, NY, to_chip, 0)
        return carry

    lax.fori_loop(0, NX, for_chips, 0)

    def key_chunk(dz):
        at = pl.ds(pl.multiple_of(((z + dz) % NZ) * CHUNK, CHUNK), CHUNK)
        act = relu[:, :, at].reshape(SLOTS, 2, 4, 16, CHUNK)
        rows = grad_rows[:, :, :, at].reshape(SLOTS, 2, 1, 16, CHUNK)
        pre = jnp.where(act > 0, rows, jnp.zeros_like(rows)).reshape(SLOTS * BLOCK, CHUNK)
        return jnp.dot(query_w[...], pre, preferred_element_type=f32)

    half = DH // 2
    part = key_chunk(4).astype(bf16)
    ring_out[0] = part
    up = send(
        ring_out.at[0, pl.ds(0, half)],
        ring_in.at[0, pl.ds(0, half)],
        ring_send.at[0],
        ring_recv.at[0],
        dev_z(1),
    )
    down = send(
        ring_out.at[0, pl.ds(half, half)],
        ring_in.at[0, pl.ds(half, half)],
        ring_send.at[1],
        ring_recv.at[1],
        dev_z(NZ - 1),
    )
    for n in (1, 2, 3):
        ahead = key_chunk(4 - n)
        up.wait()
        if n == 1:
            got = ring_in[0, 0:half, :].astype(f32)
            ahead = ahead + jnp.concatenate([got, jnp.zeros((half, CHUNK), f32)], axis=0)
        else:
            ahead = ahead + ring_in[2 * n - 3].astype(f32)
        ring_out[2 * n - 1] = ahead.astype(bf16)
        up = send(
            ring_out.at[2 * n - 1],
            ring_in.at[2 * n - 1],
            ring_send.at[2 * n],
            ring_recv.at[2 * n],
            dev_z(1),
        )
        behind = key_chunk(4 + n)
        down.wait()
        if n == 1:
            got = ring_in[0, half:DH, :].astype(f32)
            behind = behind + jnp.concatenate([jnp.zeros((half, CHUNK), f32), got], axis=0)
        else:
            behind = behind + ring_in[2 * n - 2].astype(f32)
        ring_out[2 * n] = behind.astype(bf16)
        down = send(
            ring_out.at[2 * n],
            ring_in.at[2 * n],
            ring_send.at[2 * n + 1],
            ring_recv.at[2 * n + 1],
            dev_z(NZ - 1),
        )
    own_part = key_chunk(0)

    total_g = sum_out[chip].astype(f32)
    def wait_sum(i, acc):
        pltpu.make_async_remote_copy(
            src_ref=sum_out.at[chip_at(i // NY, i % NY)],
            dst_ref=sum_in.at[i],
            send_sem=sum_send.at[i],
            recv_sem=sum_recv.at[i],
            device_id=dev_chip(i // NY, i % NY),
            device_id_type=MESH,
        ).wait()
        return acc + sum_in[i].astype(f32)

    total_g = lax.fori_loop(1, CHIPS, wait_sum, total_g)
    total_g = total_g.reshape(2, 8, 8, DH)
    for h in range(NZ):
        back_out[h, 0:8, :] = total_g[0, h]
        back_out[h, 8:16, :] = total_g[1, h]

    def start_back(i, carry):
        send(back_out.at[(z + i) % NZ], back_in.at[z], back_send.at[i], back_recv.at[i], dev_z(i))
        return carry

    lax.fori_loop(1, NZ, start_back, 0)
    back_in[pl.ds(z, 1)] = back_out[pl.ds(z, 1)]

    up.wait()
    down.wait()
    key_sum = own_part + ring_in[5].astype(f32) + ring_in[6].astype(f32)
    key_grad[...] = key_sum.T

    def wait_back(i, carry):
        pltpu.make_async_remote_copy(
            src_ref=back_out.at[(z + i) % NZ],
            dst_ref=back_in.at[(z + NZ - i) % NZ],
            send_sem=back_send.at[i],
            recv_sem=back_recv.at[i],
            device_id=dev_z(i),
            device_id_type=MESH,
        ).wait()
        return carry

    lax.fori_loop(1, NZ, wait_back, 0)
    grad = back_in[...].reshape(128, DH)
    spread = jnp.where(iota((128, 16), 0) // 8 == iota((128, 16), 1), 1.0, 0.0)
    w_rows = jnp.dot(spread, w_own, preferred_element_type=f32)
    w_rows = jnp.where(iota((128, 8), 0) % 8 == iota((128, 8), 1), w_rows, 0.0)
    w_col = jnp.sum(w_rows, axis=1, keepdims=True)
    query_grad[...] = grad * (w_col * head_scale)
    w_grad = jnp.sum(grad * query[...].astype(f32), axis=1, keepdims=True) * head_scale
    w_grad = jnp.where(iota((128, 128), 0) % 8 == iota((128, 128), 1), w_grad, 0.0)
    weight_grad[...] = jnp.sum(w_grad.reshape(16, 8, 128), axis=1)[:, 0:8]


def per_device(query, weights, keys, main_logits, row_weight, offset):
    vmem = pl.BlockSpec(memory_space=pltpu.VMEM)
    anywhere = pl.BlockSpec(memory_space=pl.ANY)
    dma = pltpu.SemaphoreType.DMA
    query_grad, key_grad, weight_grad = pl.pallas_call(
        kernel,
        out_shape=[
            jax.ShapeDtypeStruct((128, DH), f32),
            jax.ShapeDtypeStruct((CHUNK, DH), f32),
            jax.ShapeDtypeStruct((16, 8), f32),
        ],
        in_specs=[
            vmem,
            vmem,
            anywhere,
            anywhere,
            vmem,
            pl.BlockSpec(memory_space=pltpu.SMEM),
        ],
        out_specs=[vmem, vmem, vmem],
        scratch_shapes=[
            pltpu.VMEM((KEYS, DH), bf16),
            pltpu.VMEM((DH, KEYS), bf16),
            pltpu.VMEM((512, KEYS), bf16),
            pltpu.VMEM((NZ, 32, 128), bf16),
            pltpu.VMEM((NZ, 32, 128), bf16),
            pltpu.VMEM((SLOTS, BLOCK + 16, DH), bf16),
            pltpu.VMEM((SLOTS, BLOCK, KEYS), bf16),
            pltpu.VMEM((ROWS, KEYS), f32),
            pltpu.VMEM((ROWS, KEYS), f32),
            pltpu.VMEM((SLOTS, 2, 16, KEYS), bf16),
            pltpu.VMEM((DH, SLOTS * BLOCK), bf16),
            pltpu.VMEM((ROWS, 128), f32),
            pltpu.VMEM((3, 8, 128), f32),
            pltpu.VMEM((7, 8, 128), f32),
            pltpu.VMEM((CHIPS, BLOCK, DH), bf16),
            pltpu.VMEM((CHIPS, BLOCK, DH), bf16),
            pltpu.VMEM((CHIPS, BLOCK, DH), bf16),
            pltpu.VMEM((CHIPS, BLOCK, DH), bf16),
            pltpu.VMEM((7, DH, CHUNK), bf16),
            pltpu.VMEM((7, DH, CHUNK), bf16),
            pltpu.VMEM((NZ, 16, DH), f32),
            pltpu.VMEM((NZ, 16, DH), f32),
            dma((2,)),
            dma((NZ,)),
            dma((NZ,)),
            dma((CHIPS,)),
            dma((CHIPS,)),
            dma((CHIPS,)),
            dma((CHIPS,)),
            dma((7,)),
            dma((7,)),
            dma((CHIPS // GROUP,)),
            dma((CHIPS // GROUP,)),
            dma((CHIPS,)),
            dma((CHIPS,)),
            dma((8,)),
            dma((8,)),
            dma((NZ,)),
            dma((NZ,)),
        ],
        compiler_params=pltpu.CompilerParams(
            collective_id=0, has_side_effects=True, vmem_limit_bytes=56 * 2**20
        ),
    )(
        query.reshape(128, DH),
        weights,
        keys,
        main_logits,
        row_weight.reshape(1, 512),
        offset,
    )
    return query_grad.reshape(16, 8, DH), key_grad, weight_grad


def solution(mesh):
    in_specs = (P("ctx", "head", None), P("ctx", "head"), P("ctx", None), P(None, "ctx"), P(), P())
    out_specs = (P("ctx", "head", None), P(("ctx", "head"), None), P("ctx", "head"))
    return jax.shard_map(
        per_device, mesh=mesh, in_specs=in_specs, out_specs=out_specs, check_vma=False
    )
```

```python
import functools

import jax
import jax.numpy as jnp
from jax import lax
from jax.experimental import pallas as pl
from jax.experimental.pallas import tpu as pltpu
from jax.sharding import PartitionSpec as P

MESH = pl.DeviceIdType.MESH
masked_value = -1e30
bf16 = jnp.bfloat16
f32 = jnp.float32

NX, NY, NZ = 4, 4, 8
CHIPS = NX * NY
ROWS = 2 * CHIPS
KEYS = 2048
BOTH = 2 * KEYS
DH = 128
BLOCK = 128
GROUP = 4
CHUNK = 256
NCHUNK = BOTH // CHUNK


def iota(shape, dim):
    return lax.broadcasted_iota(jnp.int32, shape, dim)


def fold_rows(tiles):
    sub = iota(tiles[0].shape, 0)
    for k in (4, 2, 1):
        low = (sub & k) == 0
        half = len(tiles) // 2
        out = []
        for a, b in zip(tiles[:half], tiles[half:]):
            out.append(
                jnp.where(low, a + pltpu.roll(a, 8 - k, 0), b + pltpu.roll(b, k, 0))
            )
        tiles = out
    return tiles[0]


def copy_of(src, dst, send_sem, recv_sem, device):
    return pltpu.make_async_remote_copy(
        src_ref=src,
        dst_ref=dst,
        send_sem=send_sem,
        recv_sem=recv_sem,
        device_id=device,
        device_id_type=MESH,
    )


def kernel(
    query_hbm,
    weights_hbm,
    keys_hbm,
    logits_hbm,
    row_weight,
    offset,
    back,
    key_sum,
    query,
    weights,
    keys,
    keys_t,
    logits,
    own_logits,
    sib_logits,
    send_a,
    recv_a,
    slots,
    relu,
    score,
    target,
    grad_rows,
    query_w,
    row_scale,
    stat_in,
    sum_out,
    sum_in,
    key_own,
    key_sib_out,
    key_sib_in,
    key_out,
    key_in,
    back_out,
    back_in,
    local_sem,
    a_send,
    a_recv,
    k_send,
    k_recv,
    g_send,
    g_recv,
    st_send,
    st_recv,
    sum_send,
    sum_recv,
    sib_send,
    sib_recv,
    key_send,
    key_recv,
    back_send,
    back_recv,
):
    ctx = lax.axis_index("ctx")
    z = lax.axis_index("head")
    core = ctx % 2
    chip = ctx // 2
    x = chip // NY
    y = chip % NY
    head_scale = DH**-0.5
    loss_scale = float(KEYS * 2 * CHIPS) ** 0.5

    def chip_at(dx, dy):
        return ((x + dx) % NX) * NY + (y + dy) % NY

    def dev_chip(dx, dy):
        return {"ctx": chip_at(dx, dy) * 2 + core, "head": z}

    def dev_z(dz):
        return {"ctx": ctx, "head": (z + dz) % NZ}

    sibling = {"ctx": chip * 2 + (1 - core), "head": z}

    load_query = pltpu.make_async_copy(query_hbm, query, local_sem.at[0])
    load_query.start()
    load_weights = pltpu.make_async_copy(weights_hbm, weights, local_sem.at[1])
    load_weights.start()
    own_keys = keys.at[pl.ds(core * KEYS, KEYS)]
    load_keys = pltpu.make_async_copy(keys_hbm, own_keys, local_sem.at[2])
    load_keys.start()
    load_logits = pltpu.make_async_copy(logits_hbm, logits, local_sem.at[3])
    load_logits.start()
    barrier = pltpu.get_barrier_semaphore()

    def greet_z(i, carry):
        pl.semaphore_signal(barrier, inc=1, device_id=dev_z(i), device_id_type=MESH)
        return carry

    lax.fori_loop(1, NZ, greet_z, 0)

    def greet(i, carry):
        pl.semaphore_signal(
            barrier, inc=1, device_id=dev_chip(i // NY, i % NY), device_id_type=MESH
        )
        return carry

    lax.fori_loop(1, CHIPS, greet, 0)
    pl.semaphore_signal(barrier, inc=1, device_id=sibling, device_id_type=MESH)

    lane = iota((8, 128), 1)
    place = jnp.where(
        (lane % 8 == iota((8, 128), 0)) & ((lane % 64) // 8 == z), 1.0, 0.0
    ).astype(f32)
    pair = iota((16, 128), 0) % 2 == iota((16, 128), 1) // 64
    load_weights.wait()
    w_spread = lax.dot_general(
        weights[...].astype(f32), place, (((0,), (0,)), ((), ())), preferred_element_type=f32
    )
    w_spread = jnp.where(pair, w_spread, 0.0)
    load_query.wait()
    for to in range(NZ):
        send_a[to, 0:16, :] = query[16 * to : 16 * to + 16, :]
        row = w_spread[2 * to : 2 * to + 1, :] + w_spread[2 * to + 1 : 2 * to + 2, :]
        send_a[to, 16:32, :] = jnp.broadcast_to(row, (16, 128)).astype(bf16)
    pl.semaphore_wait(barrier, CHIPS - 1 + NZ - 1 + 1)

    def a_copy(i):
        return copy_of(
            send_a.at[(z + i) % NZ], recv_a.at[z], a_send.at[i], a_recv.at[i], dev_z(i)
        )

    def start_a(i, carry):
        a_copy(i).start()
        return carry

    lax.fori_loop(1, NZ, start_a, 0)
    recv_a[pl.ds(z, 1)] = send_a[pl.ds(z, 1)]

    load_keys.wait()
    share_keys = copy_of(own_keys, own_keys, k_send.at[0], k_recv.at[0], sibling)
    share_keys.start()

    def transpose_keys(first):
        for i in range(KEYS // 256):
            at = pl.ds(pl.multiple_of(first * KEYS + 256 * i, 256), 256)
            keys_t[:, at] = keys[at, :].astype(f32).T.astype(bf16)

    transpose_keys(core)

    def wait_a(i, carry):
        copy_of(
            send_a.at[(z + i) % NZ],
            recv_a.at[(z + NZ - i) % NZ],
            a_send.at[i],
            a_recv.at[i],
            dev_z(i),
        ).wait()
        return carry

    lax.fori_loop(1, NZ, wait_a, 0)
    got = recv_a[...].astype(f32)
    mine = got[:, 0:16, :].reshape(8, 2, 8, DH)
    own = jnp.concatenate([mine[:, 0].reshape(64, DH), mine[:, 1].reshape(64, DH)], axis=0)
    own_w = jnp.sum(got[:, 16:32, :], axis=0)
    slots[pl.ds(chip, 1), 0:BLOCK, :] = own.astype(bf16)[None]
    slots[pl.ds(chip, 1), BLOCK : BLOCK + 16, :] = own_w.astype(bf16)[None]

    def near_first(n):
        return n + (n // 2) * (1 - 2 * (n % 2))

    def start_g(m, carry):
        dx = near_first(m // NY)
        dy = near_first(m % NY)
        i = dx * NY + dy
        copy_of(
            slots.at[chip], slots.at[chip], g_send.at[i], g_recv.at[i], dev_chip(dx, dy)
        ).start()
        return carry

    lax.fori_loop(1, CHIPS, start_g, 0)

    def row_of(shape, of_core):
        r = iota(shape, 0)
        slot = (r // 8) * 4 + r % 4
        return 16 * (slot * 2 + of_core) + 2 * z + (r // 4) % 2

    here = row_of((ROWS, 512), core) == iota((ROWS, 512), 1)
    there = row_of((ROWS, 512), 1 - core) == iota((ROWS, 512), 1)
    rw_col = jnp.sum(jnp.where(here, row_weight[...], 0.0), axis=1, keepdims=True)
    row_scale[...] = jnp.broadcast_to(rw_col * loss_scale, (ROWS, 128))
    load_logits.wait()
    pick = jnp.where(there, 1.0, 0.0).astype(bf16)
    sib_logits[...] = jnp.dot(pick, logits[...], preferred_element_type=f32).astype(bf16)
    share_logits = copy_of(
        sib_logits, own_logits.at[core], k_send.at[1], k_recv.at[1], sibling
    )
    share_logits.start()
    pick = jnp.where(here, 1.0, 0.0).astype(bf16)
    own_logits[pl.ds(core, 1)] = jnp.dot(
        pick, logits[...], preferred_element_type=f32
    ).astype(bf16)[None]
    share_keys.wait()
    transpose_keys(1 - core)
    limit = offset[0] - chip * BOTH

    def is_allowed():
        return iota((ROWS, BOTH), 1) <= limit + row_of((ROWS, BOTH), core)

    share_logits.wait()
    tlogits = jnp.concatenate([own_logits[0], own_logits[1]], axis=1).astype(f32)
    tmasked = jnp.where(is_allowed(), tlogits, masked_value)
    tpeak = jnp.max(tmasked, axis=1, keepdims=True)
    texp = jnp.where(is_allowed(), jnp.exp(tmasked - tpeak), 0.0)
    target[...] = texp
    ttotal = jnp.sum(texp, axis=1, keepdims=True)

    def forward(m, carry):
        dx = near_first(m)
        gi = (x + NX - dx) % NX

        def arrive(dy, c2):
            i = dx * NY + dy

            @pl.when(i > 0)
            def _():
                copy_of(
                    slots.at[chip],
                    slots.at[chip_at(NX - dx, NY - dy)],
                    g_send.at[i],
                    g_recv.at[i],
                    dev_chip(dx, dy),
                ).wait()

            return c2

        lax.fori_loop(0, NY, arrive, 0)
        block = slots[pl.ds(gi * GROUP, GROUP)]
        q = block[:, 0:BLOCK, :].reshape(GROUP * BLOCK, DH)
        w_tiles = []
        for i in range(GROUP):
            w_row = block[i, BLOCK : BLOCK + 16, :].astype(f32)[0:1] * head_scale
            w_col = jnp.broadcast_to(w_row, (128, 128)).T
            w_tiles.append(w_col.reshape(2, 8, 8, 128))
            qw = block[i, 0:BLOCK, :].astype(f32) * w_col
            query_w[:, pl.ds(pl.multiple_of((gi * GROUP + i) * 128, 128), 128)] = qw.T.astype(bf16)
        for c in range(NCHUNK):
            at = slice(c * CHUNK, (c + 1) * CHUNK)
            dotted = jnp.dot(q, keys_t[:, at], preferred_element_type=f32)
            active = jnp.maximum(dotted, 0.0)
            relu[pl.ds(gi * GROUP, GROUP), :, at] = active.reshape(GROUP, BLOCK, CHUNK).astype(bf16)
            active = active.reshape(GROUP, 2, 8, 8, CHUNK)
            for l in range(CHUNK // 128):
                tiles = []
                for j in range(2):
                    for i in range(GROUP):
                        part = active[i, j, :, :, l * 128 : l * 128 + 128] * w_tiles[i][j]
                        tiles.append(jnp.sum(part, axis=0))
                score[
                    pl.ds(pl.multiple_of(gi * 8, 8), 8),
                    c * CHUNK + l * 128 : c * CHUNK + l * 128 + 128,
                ] = fold_rows(tiles)
        return carry

    lax.fori_loop(0, NX, forward, 0)

    masked = jnp.where(is_allowed(), score[...], masked_value)
    peak = jnp.max(masked, axis=1, keepdims=True)
    exps = jnp.where(is_allowed(), jnp.exp(masked - peak), 0.0)
    score[...] = exps
    total = jnp.sum(exps, axis=1, keepdims=True)
    lane = iota((ROWS, 128), 1)
    stats = jnp.where(
        lane == 0,
        peak,
        jnp.where(lane == 1, total, jnp.where(lane == 2, tpeak, jnp.where(lane == 3, ttotal, 0.0))),
    )
    local = jnp.concatenate([stats, jnp.zeros((128 - ROWS, 128), f32)], axis=0).T[0:8]
    stat_in[0] = local

    def stat_copy(i):
        return copy_of(
            stat_in.at[0], stat_in.at[i], st_send.at[i], st_recv.at[i], dev_chip(i // NY, i % NY)
        )

    def start_stat(i, carry):
        stat_copy(i).start()
        return carry

    lax.fori_loop(1, CHIPS, start_stat, 0)

    def wait_stat(i, carry):
        stat_copy(i).wait()
        return carry

    lax.fori_loop(1, CHIPS, wait_stat, 0)
    every = [stat_in[i] for i in range(CHIPS)]
    top = functools.reduce(jnp.maximum, every)
    total = sum(s * pltpu.roll(jnp.exp(s - top), 1, 0) for s in every)
    total = jnp.where(iota((8, 128), 0) < 4, total, 1.0)
    shares = jnp.exp(local - top) / pltpu.roll(total, 7, 0)
    shares = jnp.concatenate([shares, jnp.zeros((120, 128), f32)], axis=0).T[0:ROWS]
    prob_scale = shares[:, 0:1] * row_scale[:, 0:1]
    target_scale = shares[:, 2:3] * row_scale[:, 0:1]
    score[...] = score[...] * prob_scale - target[...] * target_scale
    for i in range(NX):
        for j in range(2):
            for k in range(GROUP):
                row = score[i * 8 + j * 4 + k : i * 8 + j * 4 + k + 1, :]
                grad_rows[i * GROUP + k, j] = jnp.broadcast_to(row, (16, BOTH)).astype(bf16)

    def key_place(n):
        return (1 - n % 2) * (4 + n // 2) + (n % 2) * ((7 - n) // 2)

    def key_chunk(of_core, dz):
        first = of_core * KEYS + ((z + dz) % NZ) * CHUNK
        at = pl.ds(pl.multiple_of(first, CHUNK), CHUNK)
        act = relu[:, :, at].reshape(CHIPS, 2, 4, 16, CHUNK)
        rows = grad_rows[:, :, :, at].reshape(CHIPS, 2, 1, 16, CHUNK)
        pre = jnp.where(act > 0, rows, jnp.zeros_like(rows)).reshape(CHIPS * BLOCK, CHUNK)
        return jnp.dot(query_w[...], pre, preferred_element_type=f32)

    def sib_copy(n):
        return copy_of(
            key_sib_out.at[n], key_sib_in.at[n], sib_send.at[n], sib_recv.at[n], sibling
        )

    def key_copy(n):
        return copy_of(
            key_out.at[n], key_in.at[n], key_send.at[n], key_recv.at[n], dev_z(key_place(n))
        )

    def key_pass_on(n):
        sib_copy(n).wait()
        key_out[n] = (key_own[n] + key_sib_in[n].astype(f32)).astype(bf16)
        key_copy(n).start()

    def key_step(n, carry):
        theirs = key_chunk(1 - core, key_place(n))
        ours = key_chunk(core, key_place(n))
        key_sib_out[n] = theirs.astype(bf16)
        sib_copy(n).start()
        key_own[n] = ours

        @pl.when((n != 0) & (n != 3))
        def _():
            key_pass_on(n - 1)

        return carry

    lax.fori_loop(0, 3, key_step, 0)

    def backward_query(gi):
        acc = jnp.zeros((GROUP * BLOCK, DH), f32)
        for c in range(NCHUNK):
            at = slice(c * CHUNK, (c + 1) * CHUNK)
            act = relu[pl.ds(gi * GROUP, GROUP), :, at].reshape(GROUP, 2, 4, 16, CHUNK)
            rows = grad_rows[pl.ds(gi * GROUP, GROUP), :, :, at].reshape(GROUP, 2, 1, 16, CHUNK)
            pre = jnp.where(act > 0, rows, jnp.zeros_like(rows)).reshape(GROUP * BLOCK, CHUNK)
            acc = acc + jnp.dot(pre, keys[at, :], preferred_element_type=f32)
        return acc.reshape(GROUP, BLOCK, DH)

    def sum_copy(dx, dy):
        i = dx * NY + dy
        return copy_of(
            sum_out.at[chip_at(dx, dy)],
            sum_in.at[i],
            sum_send.at[i],
            sum_recv.at[i],
            dev_chip(dx, dy),
        )

    def backward(n, carry):
        dx = 2 - n + (n // 2) * (3 - 2 * (n % 2))
        g = (x + dx) % NX
        sum_out[pl.ds(g * GROUP, GROUP)] = backward_query(g).astype(bf16)

        def to_chip(dy, c2):
            @pl.when(dx * NY + dy > 0)
            def _():
                sum_copy(dx, dy).start()

            return c2

        lax.fori_loop(0, NY, to_chip, 0)

        @pl.when(n == 0)
        def _():
            key_pass_on(2)

        return carry

    lax.fori_loop(0, NX, backward, 0)
    lax.fori_loop(3, NZ, key_step, 0)

    def wait_sum(i, acc):
        sum_copy(i // NY, i % NY).wait()
        return acc + sum_in[i].astype(f32)

    total_g = lax.fori_loop(1, CHIPS, wait_sum, sum_out[chip].astype(f32))
    total_g = total_g.reshape(2, 8, 8, DH)
    for h in range(NZ):
        back_out[h, 0:8, :] = total_g[0, h]
        back_out[h, 8:16, :] = total_g[1, h]

    def start_back(i, carry):
        copy_of(
            back_out.at[(z + i) % NZ], back_in.at[z], back_send.at[i], back_recv.at[i], dev_z(i)
        ).start()
        return carry

    lax.fori_loop(1, NZ, start_back, 0)
    back_in[pl.ds(z, 1)] = back_out[pl.ds(z, 1)]

    sib_copy(NZ - 1).wait()

    def wait_key(n, acc):
        key_copy(n).wait()
        return acc + key_in[n].astype(f32)

    acc = key_own[NZ - 1] + key_sib_in[NZ - 1].astype(f32)
    key_sum[...] = lax.fori_loop(0, NZ - 1, wait_key, acc).T

    def wait_back(i, carry):
        copy_of(
            back_out.at[(z + i) % NZ],
            back_in.at[(z + NZ - i) % NZ],
            back_send.at[i],
            back_recv.at[i],
            dev_z(i),
        ).wait()
        return carry

    lax.fori_loop(1, NZ, wait_back, 0)
    back[...] = back_in[...].reshape(128, DH)


def finish(back, key_sum, query, weights, query_grad, key_grad, weight_grad):
    head_scale = DH**-0.5
    key_grad[...] = key_sum[...]
    grad = back[...] * head_scale
    spread = jnp.where(iota((16, 128), 0) == iota((16, 128), 1) // 8, 1.0, 0.0)
    w_rows = lax.dot_general(
        spread,
        weights[...].astype(f32),
        (((0,), (1,)), ((), ())),
        preferred_element_type=f32,
    )
    w_rows = jnp.where(iota((128, 8), 0) % 8 == iota((128, 8), 1), w_rows, 0.0)
    query_grad[...] = grad * jnp.sum(w_rows, axis=1, keepdims=True)
    w_grad = jnp.sum(grad * query[...].astype(f32), axis=1, keepdims=True).reshape(16, 8, 1)
    out = jnp.zeros((8, 128), f32)
    for t in range(16):
        out = jnp.where(iota((8, 128), 1) == t, w_grad[t], out)
    weight_grad[...] = out[:, 0:16]


def per_device(query, weights, keys, main_logits, row_weight, offset):
    vmem = pl.BlockSpec(memory_space=pltpu.VMEM)
    anywhere = pl.BlockSpec(memory_space=pl.ANY)
    dma = pltpu.SemaphoreType.DMA
    query = query.reshape(128, DH)
    weights = weights.T
    back, key_sum = pl.pallas_call(
        kernel,
        out_shape=[
            jax.ShapeDtypeStruct((128, DH), f32),
            jax.ShapeDtypeStruct((CHUNK, DH), f32),
        ],
        in_specs=[
            anywhere,
            anywhere,
            anywhere,
            anywhere,
            vmem,
            pl.BlockSpec(memory_space=pltpu.SMEM),
        ],
        out_specs=[vmem, vmem],
        scratch_shapes=[
            pltpu.VMEM((128, DH), bf16),
            pltpu.VMEM((8, 16), bf16),
            pltpu.VMEM((BOTH, DH), bf16),
            pltpu.VMEM((DH, BOTH), bf16),
            pltpu.VMEM((512, KEYS), bf16),
            pltpu.VMEM((2, ROWS, KEYS), bf16),
            pltpu.VMEM((ROWS, KEYS), bf16),
            pltpu.VMEM((NZ, 32, 128), bf16),
            pltpu.VMEM((NZ, 32, 128), bf16),
            pltpu.VMEM((CHIPS, BLOCK + 16, DH), bf16),
            pltpu.VMEM((CHIPS, BLOCK, BOTH), bf16),
            pltpu.VMEM((ROWS, BOTH), f32),
            pltpu.VMEM((ROWS, BOTH), f32),
            pltpu.VMEM((CHIPS, 2, 16, BOTH), bf16),
            pltpu.VMEM((DH, CHIPS * BLOCK), bf16),
            pltpu.VMEM((ROWS, 128), f32),
            pltpu.VMEM((CHIPS, 8, 128), f32),
            pltpu.VMEM((CHIPS, BLOCK, DH), bf16),
            pltpu.VMEM((CHIPS, BLOCK, DH), bf16),
            pltpu.VMEM((NZ, DH, CHUNK), f32),
            pltpu.VMEM((NZ, DH, CHUNK), bf16),
            pltpu.VMEM((NZ, DH, CHUNK), bf16),
            pltpu.VMEM((NZ, DH, CHUNK), bf16),
            pltpu.VMEM((NZ, DH, CHUNK), bf16),
            pltpu.VMEM((NZ, 16, DH), f32),
            pltpu.VMEM((NZ, 16, DH), f32),
            dma((4,)),
            dma((NZ,)),
            dma((NZ,)),
            dma((2,)),
            dma((2,)),
            dma((CHIPS,)),
            dma((CHIPS,)),
            dma((CHIPS,)),
            dma((CHIPS,)),
            dma((CHIPS,)),
            dma((CHIPS,)),
            dma((NZ,)),
            dma((NZ,)),
            dma((NZ,)),
            dma((NZ,)),
            dma((NZ,)),
            dma((NZ,)),
        ],
        compiler_params=pltpu.CompilerParams(
            collective_id=0, has_side_effects=True, vmem_limit_bytes=56 * 2**20
        ),
    )(
        query,
        weights,
        keys,
        main_logits,
        row_weight.reshape(1, 512),
        offset,
    )
    query_grad, key_grad, weight_grad = pl.pallas_call(
        finish,
        out_shape=[
            jax.ShapeDtypeStruct((128, DH), f32),
            jax.ShapeDtypeStruct((CHUNK, DH), f32),
            jax.ShapeDtypeStruct((8, 16), f32),
        ],
        in_specs=[vmem] * 4,
        out_specs=[vmem] * 3,
    )(back, key_sum, query, weights)
    return query_grad.reshape(16, 8, DH), key_grad, weight_grad.T


def solution(mesh):
    in_specs = (P("ctx", "head", None), P("ctx", "head"), P("ctx", None), P(None, "ctx"), P(), P())
    out_specs = (P("ctx", "head", None), P(("ctx", "head"), None), P("ctx", "head"))
    return jax.shard_map(
        per_device, mesh=mesh, in_specs=in_specs, out_specs=out_specs, check_vma=False
    )
```

```python
import functools

import jax
import jax.numpy as jnp
from jax import lax
from jax.experimental import pallas as pl
from jax.experimental.pallas import tpu as pltpu
from jax.sharding import PartitionSpec as P

MESH = pl.DeviceIdType.MESH
masked_value = -1e30
bf16 = jnp.bfloat16
f32 = jnp.float32

NX, NY, NZ = 4, 4, 8
CHIPS = NX * NY
ROWS = 2 * CHIPS
KEYS = 2048
BOTH = 2 * KEYS
DH = 128
BLOCK = 128
GROUP = 4
CHUNK = 256
NCHUNK = BOTH // CHUNK
LAG = 2
WHEN = 1
EARLY = 4


def iota(shape, dim):
    return lax.broadcasted_iota(jnp.int32, shape, dim)


def fold_rows(tiles):
    sub = iota(tiles[0].shape, 0)
    for k in (4, 2, 1):
        low = (sub & k) == 0
        half = len(tiles) // 2
        out = []
        for a, b in zip(tiles[:half], tiles[half:]):
            out.append(
                jnp.where(low, a + pltpu.roll(a, 8 - k, 0), b + pltpu.roll(b, k, 0))
            )
        tiles = out
    return tiles[0]


def copy_of(src, dst, send_sem, recv_sem, device):
    return pltpu.make_async_remote_copy(
        src_ref=src,
        dst_ref=dst,
        send_sem=send_sem,
        recv_sem=recv_sem,
        device_id=device,
        device_id_type=MESH,
    )


def kernel(
    query_hbm,
    weights_hbm,
    keys_hbm,
    logits_hbm,
    row_weight,
    offset,
    back,
    key_sum,
    query,
    weights,
    keys,
    keys_t,
    logits,
    own_logits,
    sib_logits,
    send_a,
    recv_a,
    slots,
    relu,
    score,
    target,
    query_w,
    row_scale,
    stat_in,
    sum_out,
    sum_in,
    key_own,
    key_sib_out,
    key_sib_in,
    key_out,
    key_in,
    back_out,
    back_in,
    local_sem,
    a_send,
    a_recv,
    k_send,
    k_recv,
    g_send,
    g_recv,
    st_send,
    st_recv,
    sum_send,
    sum_recv,
    sib_send,
    sib_recv,
    key_send,
    key_recv,
    back_send,
    back_recv,
):
    ctx = lax.axis_index("ctx")
    z = lax.axis_index("head")
    core = ctx % 2
    chip = ctx // 2
    x = chip // NY
    y = chip % NY
    head_scale = DH**-0.5
    loss_scale = float(KEYS * 2 * CHIPS) ** 0.5

    def chip_at(dx, dy):
        return ((x + dx) % NX) * NY + (y + dy) % NY

    def dev_chip(dx, dy):
        return {"ctx": chip_at(dx, dy) * 2 + core, "head": z}

    def dev_z(dz):
        return {"ctx": ctx, "head": (z + dz) % NZ}

    sibling = {"ctx": chip * 2 + (1 - core), "head": z}

    load_query = pltpu.make_async_copy(query_hbm, query, local_sem.at[0])
    load_query.start()
    load_weights = pltpu.make_async_copy(weights_hbm, weights, local_sem.at[1])
    load_weights.start()
    own_keys = keys.at[pl.ds(core * KEYS, KEYS)]
    load_keys = pltpu.make_async_copy(keys_hbm, own_keys, local_sem.at[2])
    load_keys.start()
    load_logits = pltpu.make_async_copy(logits_hbm, logits, local_sem.at[3])
    load_logits.start()
    barrier = pltpu.get_barrier_semaphore()

    def greet_z(i, carry):
        pl.semaphore_signal(barrier, inc=1, device_id=dev_z(i), device_id_type=MESH)
        return carry

    lax.fori_loop(1, NZ, greet_z, 0)

    def greet(i, carry):
        pl.semaphore_signal(
            barrier, inc=1, device_id=dev_chip(i // NY, i % NY), device_id_type=MESH
        )
        return carry

    lax.fori_loop(1, CHIPS, greet, 0)
    pl.semaphore_signal(barrier, inc=1, device_id=sibling, device_id_type=MESH)

    lane = iota((8, 128), 1)
    place = jnp.where(
        (lane % 8 == iota((8, 128), 0)) & ((lane % 64) // 8 == z), 1.0, 0.0
    ).astype(f32)
    pair = iota((16, 128), 0) % 2 == iota((16, 128), 1) // 64
    load_weights.wait()
    w_spread = lax.dot_general(
        weights[...].astype(f32), place, (((0,), (0,)), ((), ())), preferred_element_type=f32
    )
    w_spread = jnp.where(pair, w_spread, 0.0)
    load_query.wait()
    for to in range(NZ):
        send_a[to, 0:16, :] = query[16 * to : 16 * to + 16, :]
        row = w_spread[2 * to : 2 * to + 1, :] + w_spread[2 * to + 1 : 2 * to + 2, :]
        send_a[to, 16:32, :] = jnp.broadcast_to(row, (16, 128)).astype(bf16)
    pl.semaphore_wait(barrier, CHIPS - 1 + NZ - 1 + 1)

    def a_copy(i):
        return copy_of(
            send_a.at[(z + i) % NZ], recv_a.at[z], a_send.at[i], a_recv.at[i], dev_z(i)
        )

    def start_a(i, carry):
        a_copy(i).start()
        return carry

    lax.fori_loop(1, NZ, start_a, 0)
    recv_a[pl.ds(z, 1)] = send_a[pl.ds(z, 1)]

    load_keys.wait()
    share_keys = copy_of(own_keys, own_keys, k_send.at[0], k_recv.at[0], sibling)
    share_keys.start()

    def transpose_keys(first):
        for i in range(KEYS // 256):
            at = pl.ds(pl.multiple_of(first * KEYS + 256 * i, 256), 256)
            keys_t[:, at] = keys[at, :].astype(f32).T.astype(bf16)

    transpose_keys(core)

    def wait_a(i, carry):
        copy_of(
            send_a.at[(z + i) % NZ],
            recv_a.at[(z + NZ - i) % NZ],
            a_send.at[i],
            a_recv.at[i],
            dev_z(i),
        ).wait()
        return carry

    lax.fori_loop(1, NZ, wait_a, 0)
    got = recv_a[...].astype(f32)
    mine = got[:, 0:16, :].reshape(8, 2, 8, DH)
    own = jnp.concatenate([mine[:, 0].reshape(64, DH), mine[:, 1].reshape(64, DH)], axis=0)
    own_w = jnp.sum(got[:, 16:32, :], axis=0)
    slots[pl.ds(chip, 1), 0:BLOCK, :] = own.astype(bf16)[None]
    slots[pl.ds(chip, 1), BLOCK : BLOCK + 16, :] = own_w.astype(bf16)[None]

    def near_first(n):
        return n + (n // 2) * (1 - 2 * (n % 2))

    def start_g(m, carry):
        dx = near_first(m // NY)
        dy = near_first(m % NY)
        i = dx * NY + dy
        copy_of(
            slots.at[chip], slots.at[chip], g_send.at[i], g_recv.at[i], dev_chip(dx, dy)
        ).start()
        return carry

    lax.fori_loop(1, CHIPS, start_g, 0)

    def row_of(shape, of_core):
        r = iota(shape, 0)
        slot = (r // 8) * 4 + r % 4
        return 16 * (slot * 2 + of_core) + 2 * z + (r // 4) % 2

    here = row_of((ROWS, 512), core) == iota((ROWS, 512), 1)
    there = row_of((ROWS, 512), 1 - core) == iota((ROWS, 512), 1)
    rw_col = jnp.sum(jnp.where(here, row_weight[...], 0.0), axis=1, keepdims=True)
    row_scale[...] = jnp.broadcast_to(rw_col * loss_scale, (ROWS, 128))
    load_logits.wait()
    pick = jnp.where(there, 1.0, 0.0).astype(bf16)
    sib_logits[...] = jnp.dot(pick, logits[...], preferred_element_type=f32).astype(bf16)
    share_logits = copy_of(
        sib_logits, own_logits.at[core], k_send.at[1], k_recv.at[1], sibling
    )
    share_logits.start()
    pick = jnp.where(here, 1.0, 0.0).astype(bf16)
    own_logits[pl.ds(core, 1)] = jnp.dot(
        pick, logits[...], preferred_element_type=f32
    ).astype(bf16)[None]
    share_keys.wait()
    transpose_keys(1 - core)
    limit = offset[0] - chip * BOTH

    def is_allowed():
        return iota((ROWS, BOTH), 1) <= limit + row_of((ROWS, BOTH), core)

    share_logits.wait()
    tlogits = jnp.concatenate([own_logits[0], own_logits[1]], axis=1).astype(f32)
    tmasked = jnp.where(is_allowed(), tlogits, masked_value)
    tpeak = jnp.max(tmasked, axis=1, keepdims=True)
    texp = jnp.where(is_allowed(), jnp.exp(tmasked - tpeak), 0.0)
    target[...] = texp
    ttotal = jnp.sum(texp, axis=1, keepdims=True)

    def forward(m, carry):
        dx = near_first(m)
        gi = (x + NX - dx) % NX

        def arrive(dy, c2):
            i = dx * NY + dy

            @pl.when(i > 0)
            def _():
                copy_of(
                    slots.at[chip],
                    slots.at[chip_at(NX - dx, NY - dy)],
                    g_send.at[i],
                    g_recv.at[i],
                    dev_chip(dx, dy),
                ).wait()

            return c2

        lax.fori_loop(0, NY, arrive, 0)
        block = slots[pl.ds(gi * GROUP, GROUP)]
        q = block[:, 0:BLOCK, :].reshape(GROUP * BLOCK, DH)
        w_tiles = []
        for i in range(GROUP):
            w_row = block[i, BLOCK : BLOCK + 16, :].astype(f32)[0:1] * head_scale
            w_col = jnp.broadcast_to(w_row, (128, 128)).T
            w_tiles.append(w_col.reshape(2, 8, 8, 128))
            qw = block[i, 0:BLOCK, :].astype(f32) * w_col
            query_w[:, pl.ds(pl.multiple_of((gi * GROUP + i) * 128, 128), 128)] = qw.T.astype(bf16)
        for c in range(NCHUNK):
            at = slice(c * CHUNK, (c + 1) * CHUNK)
            dotted = jnp.dot(q, keys_t[:, at], preferred_element_type=f32)
            active = jnp.maximum(dotted, 0.0)
            relu[pl.ds(gi * GROUP, GROUP), :, at] = active.reshape(GROUP, BLOCK, CHUNK).astype(bf16)
            active = active.reshape(GROUP, 2, 8, 8, CHUNK)
            for l in range(CHUNK // 128):
                tiles = []
                for j in range(2):
                    for i in range(GROUP):
                        part = active[i, j, :, :, l * 128 : l * 128 + 128] * w_tiles[i][j]
                        tiles.append(jnp.sum(part, axis=0))
                score[
                    pl.ds(pl.multiple_of(gi * 8, 8), 8),
                    c * CHUNK + l * 128 : c * CHUNK + l * 128 + 128,
                ] = fold_rows(tiles)
        return carry

    lax.fori_loop(0, NX, forward, 0)

    masked = jnp.where(is_allowed(), score[...], masked_value)
    peak = jnp.max(masked, axis=1, keepdims=True)
    exps = jnp.where(is_allowed(), jnp.exp(masked - peak), 0.0)
    score[...] = exps
    total = jnp.sum(exps, axis=1, keepdims=True)
    lane = iota((ROWS, 128), 1)
    stats = jnp.where(
        lane == 0,
        peak,
        jnp.where(lane == 1, total, jnp.where(lane == 2, tpeak, jnp.where(lane == 3, ttotal, 0.0))),
    )
    local = jnp.concatenate([stats, jnp.zeros((128 - ROWS, 128), f32)], axis=0).T[0:8]
    stat_in[0] = local

    def stat_copy(i):
        return copy_of(
            stat_in.at[0], stat_in.at[i], st_send.at[i], st_recv.at[i], dev_chip(i // NY, i % NY)
        )

    def start_stat(i, carry):
        stat_copy(i).start()
        return carry

    lax.fori_loop(1, CHIPS, start_stat, 0)

    def wait_stat(i, carry):
        stat_copy(i).wait()
        return carry

    lax.fori_loop(1, CHIPS, wait_stat, 0)
    every = [stat_in[i] for i in range(CHIPS)]
    top = functools.reduce(jnp.maximum, every)
    total = sum(s * pltpu.roll(jnp.exp(s - top), 1, 0) for s in every)
    total = jnp.where(iota((8, 128), 0) < 4, total, 1.0)
    shares = jnp.exp(local - top) / pltpu.roll(total, 7, 0)
    shares = jnp.concatenate([shares, jnp.zeros((120, 128), f32)], axis=0).T[0:ROWS]
    prob_scale = shares[:, 0:1] * row_scale[:, 0:1]
    target_scale = shares[:, 2:3] * row_scale[:, 0:1]
    score[...] = score[...] * prob_scale - target[...] * target_scale

    def key_place(n):
        return (1 - n % 2) * (4 + n // 2) + (n % 2) * ((7 - n) // 2)

    def key_chunk(of_core, dz):
        first = of_core * KEYS + ((z + dz) % NZ) * CHUNK
        at = pl.ds(pl.multiple_of(first, CHUNK), CHUNK)
        act = relu[:, :, at].reshape(CHIPS, 2, 4, 16, CHUNK)
        tile = score[:, at]
        rows = jnp.concatenate(
            [
                jnp.broadcast_to(tile[i * 8 + j * 4 + k : i * 8 + j * 4 + k + 1], (16, CHUNK))
                for i in range(NX)
                for k in range(GROUP)
                for j in range(2)
            ],
            axis=0,
        )
        rows = rows.astype(bf16).reshape(CHIPS, 2, 1, 16, CHUNK)
        pre = jnp.where(act > 0, rows, jnp.zeros_like(rows)).reshape(CHIPS * BLOCK, CHUNK)
        return jnp.dot(query_w[...], pre, preferred_element_type=f32)

    def sib_copy(n):
        return copy_of(
            key_sib_out.at[n], key_sib_in.at[n], sib_send.at[n], sib_recv.at[n], sibling
        )

    def key_copy(n):
        return copy_of(
            key_out.at[n], key_in.at[n], key_send.at[n], key_recv.at[n], dev_z(key_place(n))
        )

    def key_pass_on(n):
        sib_copy(n).wait()
        key_out[n] = (key_own[n] + key_sib_in[n].astype(f32)).astype(bf16)
        key_copy(n).start()

    def key_step(n, carry):
        theirs = key_chunk(1 - core, key_place(n))
        ours = key_chunk(core, key_place(n))
        key_sib_out[n] = theirs.astype(bf16)
        sib_copy(n).start()
        key_own[n] = ours

        @pl.when(n >= EARLY + LAG)
        def _():
            key_pass_on(n - LAG)

        return carry

    lax.fori_loop(0, EARLY, key_step, 0)

    def backward_query(gi):
        acc = jnp.zeros((GROUP * BLOCK, DH), f32)
        for c in range(NCHUNK):
            at = slice(c * CHUNK, (c + 1) * CHUNK)
            act = relu[pl.ds(gi * GROUP, GROUP), :, at].reshape(GROUP, 2, 4, 16, CHUNK)
            tile = score[pl.ds(pl.multiple_of(gi * 8, 8), 8), at]
            rows = jnp.concatenate(
                [
                    jnp.broadcast_to(tile[j * 4 + k : j * 4 + k + 1], (16, CHUNK))
                    for k in range(GROUP)
                    for j in range(2)
                ],
                axis=0,
            )
            rows = rows.astype(bf16).reshape(GROUP, 2, 1, 16, CHUNK)
            pre = jnp.where(act > 0, rows, jnp.zeros_like(rows)).reshape(GROUP * BLOCK, CHUNK)
            acc = acc + jnp.dot(pre, keys[at, :], preferred_element_type=f32)
        return acc.reshape(GROUP, BLOCK, DH)

    def sum_copy(dx, dy):
        i = dx * NY + dy
        return copy_of(
            sum_out.at[chip_at(dx, dy)],
            sum_in.at[i],
            sum_send.at[i],
            sum_recv.at[i],
            dev_chip(dx, dy),
        )

    def backward(n, carry):
        dx = 2 - n + (n // 2) * (3 - 2 * (n % 2))
        g = (x + dx) % NX
        sum_out[pl.ds(g * GROUP, GROUP)] = backward_query(g).astype(bf16)

        def to_chip(dy, c2):
            @pl.when(dx * NY + dy > 0)
            def _():
                sum_copy(dx, dy).start()

            return c2

        lax.fori_loop(0, NY, to_chip, 0)

        @pl.when(n == WHEN)
        def _():
            for k in range(EARLY):
                key_pass_on(k)

        return carry

    lax.fori_loop(0, NX, backward, 0)
    lax.fori_loop(EARLY, NZ, key_step, 0)
    for k in range(max(NZ - LAG, EARLY), NZ - 1):
        key_pass_on(k)

    def wait_sum(m, acc):
        n = m // NY
        i = (2 - n + (n // 2) * (3 - 2 * (n % 2))) * NY + NY - 1 - m % NY
        sum_copy(i // NY, i % NY).wait()
        return acc + sum_in[i].astype(f32)

    total_g = lax.fori_loop(0, CHIPS - 1, wait_sum, sum_out[chip].astype(f32))
    total_g = total_g.reshape(2, 8, 8, DH)
    for h in range(NZ):
        back_out[h, 0:8, :] = total_g[0, h]
        back_out[h, 8:16, :] = total_g[1, h]

    def start_back(i, carry):
        copy_of(
            back_out.at[(z + i) % NZ], back_in.at[z], back_send.at[i], back_recv.at[i], dev_z(i)
        ).start()
        return carry

    lax.fori_loop(1, NZ, start_back, 0)
    back_in[pl.ds(z, 1)] = back_out[pl.ds(z, 1)]

    sib_copy(NZ - 1).wait()

    def wait_key(n, acc):
        key_copy(n).wait()
        return acc + key_in[n].astype(f32)

    acc = key_own[NZ - 1] + key_sib_in[NZ - 1].astype(f32)
    key_sum[...] = lax.fori_loop(0, NZ - 1, wait_key, acc).T

    def wait_back(i, carry):
        copy_of(
            back_out.at[(z + i) % NZ],
            back_in.at[(z + NZ - i) % NZ],
            back_send.at[i],
            back_recv.at[i],
            dev_z(i),
        ).wait()
        return carry

    lax.fori_loop(1, NZ, wait_back, 0)
    back[...] = back_in[...].reshape(128, DH)


def finish(back, key_sum, query, weights, query_grad, key_grad, weight_grad):
    head_scale = DH**-0.5
    key_grad[...] = key_sum[...]
    grad = back[...] * head_scale
    spread = jnp.where(iota((16, 128), 0) == iota((16, 128), 1) // 8, 1.0, 0.0)
    w_rows = lax.dot_general(
        spread,
        weights[...].astype(f32),
        (((0,), (1,)), ((), ())),
        preferred_element_type=f32,
    )
    w_rows = jnp.where(iota((128, 8), 0) % 8 == iota((128, 8), 1), w_rows, 0.0)
    query_grad[...] = grad * jnp.sum(w_rows, axis=1, keepdims=True)
    w_grad = jnp.sum(grad * query[...].astype(f32), axis=1, keepdims=True).reshape(16, 8, 1)
    out = jnp.zeros((8, 128), f32)
    for t in range(16):
        out = jnp.where(iota((8, 128), 1) == t, w_grad[t], out)
    weight_grad[...] = out[:, 0:16]


def per_device(query, weights, keys, main_logits, row_weight, offset):
    vmem = pl.BlockSpec(memory_space=pltpu.VMEM)
    anywhere = pl.BlockSpec(memory_space=pl.ANY)
    dma = pltpu.SemaphoreType.DMA
    query = query.reshape(128, DH)
    weights = weights.T
    back, key_sum = pl.pallas_call(
        kernel,
        out_shape=[
            jax.ShapeDtypeStruct((128, DH), f32),
            jax.ShapeDtypeStruct((CHUNK, DH), f32),
        ],
        in_specs=[
            anywhere,
            anywhere,
            anywhere,
            anywhere,
            vmem,
            pl.BlockSpec(memory_space=pltpu.SMEM),
        ],
        out_specs=[vmem, vmem],
        scratch_shapes=[
            pltpu.VMEM((128, DH), bf16),
            pltpu.VMEM((8, 16), bf16),
            pltpu.VMEM((BOTH, DH), bf16),
            pltpu.VMEM((DH, BOTH), bf16),
            pltpu.VMEM((512, KEYS), bf16),
            pltpu.VMEM((2, ROWS, KEYS), bf16),
            pltpu.VMEM((ROWS, KEYS), bf16),
            pltpu.VMEM((NZ, 32, 128), bf16),
            pltpu.VMEM((NZ, 32, 128), bf16),
            pltpu.VMEM((CHIPS, BLOCK + 16, DH), bf16),
            pltpu.VMEM((CHIPS, BLOCK, BOTH), bf16),
            pltpu.VMEM((ROWS, BOTH), f32),
            pltpu.VMEM((ROWS, BOTH), f32),
            pltpu.VMEM((DH, CHIPS * BLOCK), bf16),
            pltpu.VMEM((ROWS, 128), f32),
            pltpu.VMEM((CHIPS, 8, 128), f32),
            pltpu.VMEM((CHIPS, BLOCK, DH), bf16),
            pltpu.VMEM((CHIPS, BLOCK, DH), bf16),
            pltpu.VMEM((NZ, DH, CHUNK), f32),
            pltpu.VMEM((NZ, DH, CHUNK), bf16),
            pltpu.VMEM((NZ, DH, CHUNK), bf16),
            pltpu.VMEM((NZ, DH, CHUNK), bf16),
            pltpu.VMEM((NZ, DH, CHUNK), bf16),
            pltpu.VMEM((NZ, 16, DH), f32),
            pltpu.VMEM((NZ, 16, DH), f32),
            dma((4,)),
            dma((NZ,)),
            dma((NZ,)),
            dma((2,)),
            dma((2,)),
            dma((CHIPS,)),
            dma((CHIPS,)),
            dma((CHIPS,)),
            dma((CHIPS,)),
            dma((CHIPS,)),
            dma((CHIPS,)),
            dma((NZ,)),
            dma((NZ,)),
            dma((NZ,)),
            dma((NZ,)),
            dma((NZ,)),
            dma((NZ,)),
        ],
        compiler_params=pltpu.CompilerParams(
            collective_id=0, has_side_effects=True, vmem_limit_bytes=56 * 2**20
        ),
    )(
        query,
        weights,
        keys,
        main_logits,
        row_weight.reshape(1, 512),
        offset,
    )
    query_grad, key_grad, weight_grad = pl.pallas_call(
        finish,
        out_shape=[
            jax.ShapeDtypeStruct((128, DH), f32),
            jax.ShapeDtypeStruct((CHUNK, DH), f32),
            jax.ShapeDtypeStruct((8, 16), f32),
        ],
        in_specs=[vmem] * 4,
        out_specs=[vmem] * 3,
    )(back, key_sum, query, weights)
    return query_grad.reshape(16, 8, DH), key_grad, weight_grad.T


def solution(mesh):
    in_specs = (P("ctx", "head", None), P("ctx", "head"), P("ctx", None), P(None, "ctx"), P(), P())
    out_specs = (P("ctx", "head", None), P(("ctx", "head"), None), P("ctx", "head"))
    return jax.shard_map(
        per_device, mesh=mesh, in_specs=in_specs, out_specs=out_specs, check_vma=False
    )
```

```python
import functools

import jax
import jax.numpy as jnp
from jax import lax
from jax.experimental import pallas as pl
from jax.experimental.pallas import tpu as pltpu
from jax.sharding import PartitionSpec as P

MESH = pl.DeviceIdType.MESH
masked_value = -1e30
bf16 = jnp.bfloat16
f32 = jnp.float32

NX, NY, NZ = 4, 4, 8
CHIPS = NX * NY
ROWS = 2 * CHIPS
KEYS = 2048
BOTH = 2 * KEYS
DH = 128
BLOCK = 128
GROUP = 4
CHUNK = 256
NCHUNK = BOTH // CHUNK
LAG = 2
WHEN = 1
EARLY = 4


def iota(shape, dim):
    return lax.broadcasted_iota(jnp.int32, shape, dim)


def fold_rows(tiles):
    sub = iota(tiles[0].shape, 0)
    for k in (4, 2, 1):
        low = (sub & k) == 0
        half = len(tiles) // 2
        out = []
        for a, b in zip(tiles[:half], tiles[half:]):
            out.append(
                jnp.where(low, a + pltpu.roll(a, 8 - k, 0), b + pltpu.roll(b, k, 0))
            )
        tiles = out
    return tiles[0]


def copy_of(src, dst, send_sem, recv_sem, device):
    return pltpu.make_async_remote_copy(
        src_ref=src,
        dst_ref=dst,
        send_sem=send_sem,
        recv_sem=recv_sem,
        device_id=device,
        device_id_type=MESH,
    )


def kernel(
    query_hbm,
    weights_hbm,
    keys_hbm,
    logits_hbm,
    row_weight,
    offset,
    back,
    key_sum,
    query,
    weights,
    keys,
    keys_t,
    logits,
    own_logits,
    sib_logits,
    send_a,
    recv_a,
    slots,
    relu,
    score,
    target,
    query_w,
    row_scale,
    stat_in,
    sum_out,
    sum_in,
    key_own,
    key_sib_out,
    key_sib_in,
    key_out,
    key_in,
    back_out,
    back_in,
    local_sem,
    a_send,
    a_recv,
    k_send,
    k_recv,
    g_send,
    g_recv,
    st_send,
    st_recv,
    sum_send,
    sum_recv,
    sib_send,
    sib_recv,
    key_send,
    key_recv,
    back_send,
    back_recv,
):
    ctx = lax.axis_index("ctx")
    z = lax.axis_index("head")
    core = ctx % 2
    chip = ctx // 2
    x = chip // NY
    y = chip % NY
    head_scale = DH**-0.5
    loss_scale = float(KEYS * 2 * CHIPS) ** 0.5

    def chip_at(dx, dy):
        return ((x + dx) % NX) * NY + (y + dy) % NY

    def dev_chip(dx, dy):
        return {"ctx": chip_at(dx, dy) * 2 + core, "head": z}

    def dev_z(dz):
        return {"ctx": ctx, "head": (z + dz) % NZ}

    sibling = {"ctx": chip * 2 + (1 - core), "head": z}

    load_query = pltpu.make_async_copy(query_hbm, query, local_sem.at[0])
    load_query.start()
    load_weights = pltpu.make_async_copy(weights_hbm, weights, local_sem.at[1])
    load_weights.start()
    own_keys = keys.at[pl.ds(core * KEYS, KEYS)]
    load_keys = pltpu.make_async_copy(keys_hbm, own_keys, local_sem.at[2])
    load_keys.start()
    load_logits = pltpu.make_async_copy(logits_hbm, logits, local_sem.at[3])
    load_logits.start()
    barrier = pltpu.get_barrier_semaphore()

    def far_first(n):
        return (1 - n % 2) * (4 + n // 2) + (n % 2) * ((7 - n) // 2)

    def greet_z(n, carry):
        i = far_first(n)
        pl.semaphore_signal(barrier, inc=1, device_id=dev_z(i), device_id_type=MESH)
        return carry

    lax.fori_loop(0, NZ - 1, greet_z, 0)

    def greet(i, carry):
        pl.semaphore_signal(
            barrier, inc=1, device_id=dev_chip(i // NY, i % NY), device_id_type=MESH
        )
        return carry

    lax.fori_loop(1, CHIPS, greet, 0)
    pl.semaphore_signal(barrier, inc=1, device_id=sibling, device_id_type=MESH)

    lane = iota((8, 128), 1)
    place = jnp.where(
        (lane % 8 == iota((8, 128), 0)) & ((lane % 64) // 8 == z), 1.0, 0.0
    ).astype(f32)
    pair = iota((16, 128), 0) % 2 == iota((16, 128), 1) // 64
    load_weights.wait()
    w_spread = lax.dot_general(
        weights[...].astype(f32), place, (((0,), (0,)), ((), ())), preferred_element_type=f32
    )
    w_spread = jnp.where(pair, w_spread, 0.0)
    load_query.wait()
    for to in range(NZ):
        send_a[to, 0:16, :] = query[16 * to : 16 * to + 16, :]
        row = w_spread[2 * to : 2 * to + 1, :] + w_spread[2 * to + 1 : 2 * to + 2, :]
        send_a[to, 16:32, :] = jnp.broadcast_to(row, (16, 128)).astype(bf16)
    pl.semaphore_wait(barrier, CHIPS - 1 + NZ - 1 + 1)

    def a_copy(i):
        return copy_of(
            send_a.at[(z + i) % NZ], recv_a.at[z], a_send.at[i], a_recv.at[i], dev_z(i)
        )

    def start_a(n, carry):
        a_copy(far_first(n)).start()
        return carry

    lax.fori_loop(0, NZ - 1, start_a, 0)
    recv_a[pl.ds(z, 1)] = send_a[pl.ds(z, 1)]

    load_keys.wait()
    share_keys = copy_of(own_keys, own_keys, k_send.at[0], k_recv.at[0], sibling)
    share_keys.start()

    def transpose_keys(first):
        for i in range(KEYS // 256):
            at = pl.ds(pl.multiple_of(first * KEYS + 256 * i, 256), 256)
            keys_t[:, at] = keys[at, :].astype(f32).T.astype(bf16)

    transpose_keys(core)

    def wait_a(i, carry):
        copy_of(
            send_a.at[(z + i) % NZ],
            recv_a.at[(z + NZ - i) % NZ],
            a_send.at[i],
            a_recv.at[i],
            dev_z(i),
        ).wait()
        return carry

    lax.fori_loop(1, NZ, wait_a, 0)
    got = recv_a[...].astype(f32)
    mine = got[:, 0:16, :].reshape(8, 2, 8, DH)
    own = jnp.concatenate([mine[:, 0].reshape(64, DH), mine[:, 1].reshape(64, DH)], axis=0)
    own_w = jnp.sum(got[:, 16:32, :], axis=0)
    slots[pl.ds(chip, 1), 0:BLOCK, :] = own.astype(bf16)[None]
    slots[pl.ds(chip, 1), BLOCK : BLOCK + 16, :] = own_w.astype(bf16)[None]

    def near_first(n):
        return n + (n // 2) * (1 - 2 * (n % 2))

    def start_g(m, carry):
        dx = near_first(m // NY)
        dy = near_first(m % NY)
        i = dx * NY + dy
        copy_of(
            slots.at[chip], slots.at[chip], g_send.at[i], g_recv.at[i], dev_chip(dx, dy)
        ).start()
        return carry

    lax.fori_loop(1, CHIPS, start_g, 0)

    def row_of(shape, of_core):
        r = iota(shape, 0)
        slot = (r // 8) * 4 + r % 4
        return 16 * (slot * 2 + of_core) + 2 * z + (r // 4) % 2

    here = row_of((ROWS, 512), core) == iota((ROWS, 512), 1)
    there = row_of((ROWS, 512), 1 - core) == iota((ROWS, 512), 1)
    rw_col = jnp.sum(jnp.where(here, row_weight[...], 0.0), axis=1, keepdims=True)
    row_scale[...] = jnp.broadcast_to(rw_col * loss_scale, (ROWS, 128))
    load_logits.wait()
    pick = jnp.where(there, 1.0, 0.0).astype(bf16)
    sib_logits[...] = jnp.dot(pick, logits[...], preferred_element_type=f32).astype(bf16)
    share_logits = copy_of(
        sib_logits, own_logits.at[core], k_send.at[1], k_recv.at[1], sibling
    )
    share_logits.start()
    pick = jnp.where(here, 1.0, 0.0).astype(bf16)
    own_logits[pl.ds(core, 1)] = jnp.dot(
        pick, logits[...], preferred_element_type=f32
    ).astype(bf16)[None]
    share_keys.wait()
    transpose_keys(1 - core)
    limit = offset[0] - chip * BOTH

    def is_allowed():
        return iota((ROWS, BOTH), 1) <= limit + row_of((ROWS, 1), core)

    share_logits.wait()
    tlogits = jnp.concatenate([own_logits[0], own_logits[1]], axis=1).astype(f32)
    tmasked = jnp.where(is_allowed(), tlogits, masked_value)
    tpeak = jnp.max(tmasked, axis=1, keepdims=True)
    texp = jnp.where(is_allowed(), jnp.exp(tmasked - tpeak), 0.0)
    target[...] = texp
    ttotal = jnp.sum(texp, axis=1, keepdims=True)

    def forward(m, carry):
        dx = near_first(m)
        gi = (x + NX - dx) % NX

        def arrive(dy, c2):
            i = dx * NY + dy

            @pl.when(i > 0)
            def _():
                copy_of(
                    slots.at[chip],
                    slots.at[chip_at(NX - dx, NY - dy)],
                    g_send.at[i],
                    g_recv.at[i],
                    dev_chip(dx, dy),
                ).wait()

            return c2

        lax.fori_loop(0, NY, arrive, 0)
        block = slots[pl.ds(gi * GROUP, GROUP)]
        q = block[:, 0:BLOCK, :].reshape(GROUP * BLOCK, DH)
        w_tiles = []
        for i in range(GROUP):
            w_row = block[i, BLOCK : BLOCK + 16, :].astype(f32)[0:1] * head_scale
            w_col = jnp.broadcast_to(w_row, (128, 128)).T
            w_tiles.append(w_col.reshape(2, 8, 8, 128))
            qw = block[i, 0:BLOCK, :].astype(f32) * w_col
            query_w[:, pl.ds(pl.multiple_of((gi * GROUP + i) * 128, 128), 128)] = qw.T.astype(bf16)
        for c in range(NCHUNK):
            at = slice(c * CHUNK, (c + 1) * CHUNK)
            dotted = jnp.dot(q, keys_t[:, at], preferred_element_type=f32)
            active = jnp.maximum(dotted, 0.0)
            relu[pl.ds(gi * GROUP, GROUP), :, at] = active.reshape(GROUP, BLOCK, CHUNK).astype(bf16)
            active = active.reshape(GROUP, 2, 8, 8, CHUNK)
            for l in range(CHUNK // 128):
                tiles = []
                for j in range(2):
                    for i in range(GROUP):
                        part = active[i, j, :, :, l * 128 : l * 128 + 128] * w_tiles[i][j]
                        tiles.append(jnp.sum(part, axis=0))
                score[
                    pl.ds(pl.multiple_of(gi * 8, 8), 8),
                    c * CHUNK + l * 128 : c * CHUNK + l * 128 + 128,
                ] = fold_rows(tiles)
        return carry

    lax.fori_loop(0, NX, forward, 0)

    masked = jnp.where(is_allowed(), score[...], masked_value)
    peak = jnp.max(masked, axis=1, keepdims=True)
    exps = jnp.where(is_allowed(), jnp.exp(masked - peak), 0.0)
    score[...] = exps
    total = jnp.sum(exps, axis=1, keepdims=True)
    lane = iota((ROWS, 128), 1)
    stats = jnp.where(
        lane == 0,
        peak,
        jnp.where(lane == 1, total, jnp.where(lane == 2, tpeak, jnp.where(lane == 3, ttotal, 0.0))),
    )
    local = jnp.concatenate([stats, jnp.zeros((128 - ROWS, 128), f32)], axis=0).T[0:8]
    stat_in[0] = local

    def stat_copy(i):
        return copy_of(
            stat_in.at[0], stat_in.at[i], st_send.at[i], st_recv.at[i], dev_chip(i // NY, i % NY)
        )

    def start_stat(m, carry):
        stat_copy((m + 9) % (CHIPS - 1) + 1).start()
        return carry

    lax.fori_loop(0, CHIPS - 1, start_stat, 0)

    def wait_stat(i, carry):
        stat_copy(i).wait()
        return carry

    lax.fori_loop(1, CHIPS, wait_stat, 0)
    every = [stat_in[i] for i in range(CHIPS)]
    top = functools.reduce(jnp.maximum, every)
    total = sum(s * pltpu.roll(jnp.exp(s - top), 1, 0) for s in every)
    total = jnp.where(iota((8, 128), 0) < 4, total, 1.0)
    shares = jnp.exp(local - top) / pltpu.roll(total, 7, 0)
    shares = jnp.concatenate([shares, jnp.zeros((120, 128), f32)], axis=0).T[0:ROWS]
    prob_scale = shares[:, 0:1] * row_scale[:, 0:1]
    target_scale = shares[:, 2:3] * row_scale[:, 0:1]
    score[...] = score[...] * prob_scale - target[...] * target_scale

    def key_chunk(of_core, dz):
        first = of_core * KEYS + ((z + dz) % NZ) * CHUNK
        at = pl.ds(pl.multiple_of(first, CHUNK), CHUNK)
        act = relu[:, :, at].reshape(CHIPS, 2, 4, 16, CHUNK)
        tile = score[:, at]
        rows = jnp.concatenate(
            [
                jnp.broadcast_to(tile[i * 8 + j * 4 + k : i * 8 + j * 4 + k + 1], (16, CHUNK))
                for i in range(NX)
                for k in range(GROUP)
                for j in range(2)
            ],
            axis=0,
        )
        rows = rows.astype(bf16).reshape(CHIPS, 2, 1, 16, CHUNK)
        pre = jnp.where(act > 0, rows, jnp.zeros_like(rows)).reshape(CHIPS * BLOCK, CHUNK)
        return jnp.dot(query_w[...], pre, preferred_element_type=f32)

    def sib_copy(n):
        return copy_of(
            key_sib_out.at[n], key_sib_in.at[n], sib_send.at[n], sib_recv.at[n], sibling
        )

    def key_copy(n):
        return copy_of(
            key_out.at[n], key_in.at[n], key_send.at[n], key_recv.at[n], dev_z(far_first(n))
        )

    def key_pass_on(n):
        sib_copy(n).wait()
        key_out[n] = (key_own[n] + key_sib_in[n].astype(f32)).astype(bf16)
        key_copy(n).start()

    def key_step(n, carry):
        theirs = key_chunk(1 - core, far_first(n))
        ours = key_chunk(core, far_first(n))
        key_sib_out[n] = theirs.astype(bf16)
        sib_copy(n).start()
        key_own[n] = ours

        @pl.when(n >= EARLY + LAG)
        def _():
            key_pass_on(n - LAG)

        return carry

    lax.fori_loop(0, EARLY, key_step, 0)

    def backward_query(gi):
        acc = jnp.zeros((GROUP * BLOCK, DH), f32)
        for c in range(NCHUNK):
            at = slice(c * CHUNK, (c + 1) * CHUNK)
            act = relu[pl.ds(gi * GROUP, GROUP), :, at].reshape(GROUP, 2, 4, 16, CHUNK)
            tile = score[pl.ds(pl.multiple_of(gi * 8, 8), 8), at]
            rows = jnp.concatenate(
                [
                    jnp.broadcast_to(tile[j * 4 + k : j * 4 + k + 1], (16, CHUNK))
                    for k in range(GROUP)
                    for j in range(2)
                ],
                axis=0,
            )
            rows = rows.astype(bf16).reshape(GROUP, 2, 1, 16, CHUNK)
            pre = jnp.where(act > 0, rows, jnp.zeros_like(rows)).reshape(GROUP * BLOCK, CHUNK)
            acc = acc + jnp.dot(pre, keys[at, :], preferred_element_type=f32)
        return acc.reshape(GROUP, BLOCK, DH)

    def sum_copy(dx, dy):
        i = dx * NY + dy
        return copy_of(
            sum_out.at[chip_at(dx, dy)],
            sum_in.at[i],
            sum_send.at[i],
            sum_recv.at[i],
            dev_chip(dx, dy),
        )

    def backward(n, carry):
        dx = 2 - n + (n // 2) * (3 - 2 * (n % 2))
        g = (x + dx) % NX
        sum_out[pl.ds(g * GROUP, GROUP)] = backward_query(g).astype(bf16)

        def to_chip(dy, c2):
            @pl.when(dx * NY + dy > 0)
            def _():
                sum_copy(dx, dy).start()

            return c2

        lax.fori_loop(0, NY, to_chip, 0)

        @pl.when(n == WHEN)
        def _():
            for k in range(EARLY):
                key_pass_on(k)

        return carry

    lax.fori_loop(0, NX, backward, 0)
    lax.fori_loop(EARLY, NZ, key_step, 0)

    def wait_sum(m, acc):
        n = m // NY
        i = (2 - n + (n // 2) * (3 - 2 * (n % 2))) * NY + NY - 1 - m % NY
        sum_copy(i // NY, i % NY).wait()
        return acc + sum_in[i].astype(f32)

    total_g = lax.fori_loop(0, CHIPS - 1, wait_sum, sum_out[chip].astype(f32))
    total_g = total_g.reshape(2, 8, 8, DH)
    for h in range(NZ):
        back_out[h, 0:8, :] = total_g[0, h]
        back_out[h, 8:16, :] = total_g[1, h]

    def start_back(n, carry):
        i = far_first(n)
        copy_of(
            back_out.at[(z + i) % NZ], back_in.at[z], back_send.at[i], back_recv.at[i], dev_z(i)
        ).start()
        return carry

    lax.fori_loop(0, NZ - 1, start_back, 0)
    back_in[pl.ds(z, 1)] = back_out[pl.ds(z, 1)]

    for k in range(max(NZ - LAG, EARLY), NZ - 1):
        key_pass_on(k)
    sib_copy(NZ - 1).wait()

    def wait_key(n, acc):
        key_copy(n).wait()
        return acc + key_in[n].astype(f32)

    acc = key_own[NZ - 1] + key_sib_in[NZ - 1].astype(f32)
    key_sum[...] = lax.fori_loop(0, NZ - 1, wait_key, acc).T

    def wait_back(i, carry):
        copy_of(
            back_out.at[(z + i) % NZ],
            back_in.at[(z + NZ - i) % NZ],
            back_send.at[i],
            back_recv.at[i],
            dev_z(i),
        ).wait()
        return carry

    lax.fori_loop(1, NZ, wait_back, 0)
    back[...] = back_in[...].reshape(128, DH)


def finish(back, key_sum, query, weights, query_grad, key_grad, weight_grad):
    head_scale = DH**-0.5
    key_grad[...] = key_sum[...]
    grad = back[...] * head_scale
    spread = jnp.where(iota((16, 128), 0) == iota((16, 128), 1) // 8, 1.0, 0.0)
    w_rows = lax.dot_general(
        spread,
        weights[...].astype(f32),
        (((0,), (1,)), ((), ())),
        preferred_element_type=f32,
    )
    w_rows = jnp.where(iota((128, 8), 0) % 8 == iota((128, 8), 1), w_rows, 0.0)
    query_grad[...] = grad * jnp.sum(w_rows, axis=1, keepdims=True)
    w_grad = jnp.sum(grad * query[...].astype(f32), axis=1, keepdims=True).reshape(16, 8, 1)
    out = jnp.zeros((8, 128), f32)
    for t in range(16):
        out = jnp.where(iota((8, 128), 1) == t, w_grad[t], out)
    weight_grad[...] = out[:, 0:16]


def per_device(query, weights, keys, main_logits, row_weight, offset):
    vmem = pl.BlockSpec(memory_space=pltpu.VMEM)
    anywhere = pl.BlockSpec(memory_space=pl.ANY)
    dma = pltpu.SemaphoreType.DMA
    query = query.reshape(128, DH)
    weights = weights.T
    back, key_sum = pl.pallas_call(
        kernel,
        out_shape=[
            jax.ShapeDtypeStruct((128, DH), f32),
            jax.ShapeDtypeStruct((CHUNK, DH), f32),
        ],
        in_specs=[
            anywhere,
            anywhere,
            anywhere,
            anywhere,
            vmem,
            pl.BlockSpec(memory_space=pltpu.SMEM),
        ],
        out_specs=[vmem, vmem],
        scratch_shapes=[
            pltpu.VMEM((128, DH), bf16),
            pltpu.VMEM((8, 16), bf16),
            pltpu.VMEM((BOTH, DH), bf16),
            pltpu.VMEM((DH, BOTH), bf16),
            pltpu.VMEM((512, KEYS), bf16),
            pltpu.VMEM((2, ROWS, KEYS), bf16),
            pltpu.VMEM((ROWS, KEYS), bf16),
            pltpu.VMEM((NZ, 32, 128), bf16),
            pltpu.VMEM((NZ, 32, 128), bf16),
            pltpu.VMEM((CHIPS, BLOCK + 16, DH), bf16),
            pltpu.VMEM((CHIPS, BLOCK, BOTH), bf16),
            pltpu.VMEM((ROWS, BOTH), f32),
            pltpu.VMEM((ROWS, BOTH), f32),
            pltpu.VMEM((DH, CHIPS * BLOCK), bf16),
            pltpu.VMEM((ROWS, 128), f32),
            pltpu.VMEM((CHIPS, 8, 128), f32),
            pltpu.VMEM((CHIPS, BLOCK, DH), bf16),
            pltpu.VMEM((CHIPS, BLOCK, DH), bf16),
            pltpu.VMEM((NZ, DH, CHUNK), f32),
            pltpu.VMEM((NZ, DH, CHUNK), bf16),
            pltpu.VMEM((NZ, DH, CHUNK), bf16),
            pltpu.VMEM((NZ, DH, CHUNK), bf16),
            pltpu.VMEM((NZ, DH, CHUNK), bf16),
            pltpu.VMEM((NZ, 16, DH), f32),
            pltpu.VMEM((NZ, 16, DH), f32),
            dma((4,)),
            dma((NZ,)),
            dma((NZ,)),
            dma((2,)),
            dma((2,)),
            dma((CHIPS,)),
            dma((CHIPS,)),
            dma((CHIPS,)),
            dma((CHIPS,)),
            dma((CHIPS,)),
            dma((CHIPS,)),
            dma((NZ,)),
            dma((NZ,)),
            dma((NZ,)),
            dma((NZ,)),
            dma((NZ,)),
            dma((NZ,)),
        ],
        compiler_params=pltpu.CompilerParams(
            collective_id=0, has_side_effects=True, vmem_limit_bytes=56 * 2**20
        ),
    )(
        query,
        weights,
        keys,
        main_logits,
        row_weight.reshape(1, 512),
        offset,
    )
    query_grad, key_grad, weight_grad = pl.pallas_call(
        finish,
        out_shape=[
            jax.ShapeDtypeStruct((128, DH), f32),
            jax.ShapeDtypeStruct((CHUNK, DH), f32),
            jax.ShapeDtypeStruct((8, 16), f32),
        ],
        in_specs=[vmem] * 4,
        out_specs=[vmem] * 3,
    )(back, key_sum, query, weights)
    return query_grad.reshape(16, 8, DH), key_grad, weight_grad.T


def solution(mesh):
    in_specs = (P("ctx", "head", None), P("ctx", "head"), P("ctx", None), P(None, "ctx"), P(), P())
    out_specs = (P("ctx", "head", None), P(("ctx", "head"), None), P("ctx", "head"))
    return jax.shard_map(
        per_device, mesh=mesh, in_specs=in_specs, out_specs=out_specs, check_vma=False
    )
```

```python
import functools

import jax
import jax.numpy as jnp
from jax import lax
from jax.experimental import pallas as pl
from jax.experimental.pallas import tpu as pltpu
from jax.sharding import PartitionSpec as P

MESH = pl.DeviceIdType.MESH
masked_value = -1e30
bf16 = jnp.bfloat16
f32 = jnp.float32

NX, NY, NZ = 4, 4, 8
CHIPS = NX * NY
ROWS = 2 * CHIPS
KEYS = 2048
BOTH = 2 * KEYS
DH = 128
BLOCK = 128
GROUP = 4
CHUNK = 256
NCHUNK = BOTH // CHUNK
LAG = 2
WHEN = 1
EARLY = 4


def iota(shape, dim):
    return lax.broadcasted_iota(jnp.int32, shape, dim)


def fold_rows(tiles):
    sub = iota(tiles[0].shape, 0)
    for k in (4, 2, 1):
        low = (sub & k) == 0
        half = len(tiles) // 2
        out = []
        for a, b in zip(tiles[:half], tiles[half:]):
            out.append(
                jnp.where(low, a + pltpu.roll(a, 8 - k, 0), b + pltpu.roll(b, k, 0))
            )
        tiles = out
    return tiles[0]


def copy_of(src, dst, send_sem, recv_sem, device):
    return pltpu.make_async_remote_copy(
        src_ref=src,
        dst_ref=dst,
        send_sem=send_sem,
        recv_sem=recv_sem,
        device_id=device,
        device_id_type=MESH,
    )


def kernel(
    query_hbm,
    weights_hbm,
    keys_hbm,
    logits_hbm,
    row_weight,
    offset,
    back,
    key_sum,
    query,
    weights,
    keys,
    keys_t,
    logits,
    own_logits,
    sib_logits,
    send_a,
    recv_a,
    slots,
    relu,
    score,
    target,
    query_w,
    row_scale,
    stat_in,
    sum_out,
    sum_in,
    key_own,
    key_sib_out,
    key_sib_in,
    key_out,
    key_in,
    back_out,
    back_in,
    local_sem,
    a_send,
    a_recv,
    k_send,
    k_recv,
    g_send,
    g_recv,
    st_send,
    st_recv,
    sum_send,
    sum_recv,
    sib_send,
    sib_recv,
    key_send,
    key_recv,
    back_send,
    back_recv,
):
    ctx = lax.axis_index("ctx")
    z = lax.axis_index("head")
    core = ctx % 2
    chip = ctx // 2
    x = chip // NY
    y = chip % NY
    head_scale = DH**-0.5
    loss_scale = float(KEYS * 2 * CHIPS) ** 0.5

    def chip_at(dx, dy):
        return ((x + dx) % NX) * NY + (y + dy) % NY

    def dev_chip(dx, dy):
        return {"ctx": chip_at(dx, dy) * 2 + core, "head": z}

    def dev_z(dz):
        return {"ctx": ctx, "head": (z + dz) % NZ}

    sibling = {"ctx": chip * 2 + (1 - core), "head": z}

    load_query = pltpu.make_async_copy(query_hbm, query, local_sem.at[0])
    load_query.start()
    load_weights = pltpu.make_async_copy(weights_hbm, weights, local_sem.at[1])
    load_weights.start()
    own_keys = keys.at[pl.ds(core * KEYS, KEYS)]
    load_keys = pltpu.make_async_copy(keys_hbm, own_keys, local_sem.at[2])
    load_keys.start()
    load_logits = pltpu.make_async_copy(logits_hbm, logits, local_sem.at[3])
    load_logits.start()
    barrier = pltpu.get_barrier_semaphore()

    def far_first(n):
        return (1 - n % 2) * (4 + n // 2) + (n % 2) * ((7 - n) // 2)

    def greet_z(n, carry):
        i = far_first(n)
        pl.semaphore_signal(barrier, inc=1, device_id=dev_z(i), device_id_type=MESH)
        return carry

    lax.fori_loop(0, NZ - 1, greet_z, 0)

    def greet(i, carry):
        pl.semaphore_signal(
            barrier, inc=1, device_id=dev_chip(i // NY, i % NY), device_id_type=MESH
        )
        return carry

    lax.fori_loop(1, CHIPS, greet, 0)
    pl.semaphore_signal(barrier, inc=1, device_id=sibling, device_id_type=MESH)

    lane = iota((8, 128), 1)
    place = jnp.where(
        (lane % 8 == iota((8, 128), 0)) & ((lane % 64) // 8 == z), 1.0, 0.0
    ).astype(f32)
    pair = iota((16, 128), 0) % 2 == iota((16, 128), 1) // 64
    load_weights.wait()
    w_spread = lax.dot_general(
        weights[...].astype(f32), place, (((0,), (0,)), ((), ())), preferred_element_type=f32
    )
    w_spread = jnp.where(pair, w_spread, 0.0)
    load_query.wait()
    for to in range(NZ):
        send_a[to, 0:16, :] = query[16 * to : 16 * to + 16, :]
        row = w_spread[2 * to : 2 * to + 1, :] + w_spread[2 * to + 1 : 2 * to + 2, :]
        send_a[to, 16:32, :] = jnp.broadcast_to(row, (16, 128)).astype(bf16)
    pl.semaphore_wait(barrier, CHIPS - 1 + NZ - 1 + 1)

    def a_copy(i):
        return copy_of(
            send_a.at[(z + i) % NZ], recv_a.at[z], a_send.at[i], a_recv.at[i], dev_z(i)
        )

    def start_a(n, carry):
        a_copy(far_first(n)).start()
        return carry

    lax.fori_loop(0, NZ - 1, start_a, 0)
    recv_a[pl.ds(z, 1)] = send_a[pl.ds(z, 1)]

    load_keys.wait()
    share_keys = copy_of(own_keys, own_keys, k_send.at[0], k_recv.at[0], sibling)
    share_keys.start()

    def transpose_keys(first):
        for i in range(KEYS // 256):
            at = pl.ds(pl.multiple_of(first * KEYS + 256 * i, 256), 256)
            keys_t[:, at] = keys[at, :].astype(f32).T.astype(bf16)

    transpose_keys(core)

    def wait_a(i, carry):
        copy_of(
            send_a.at[(z + i) % NZ],
            recv_a.at[(z + NZ - i) % NZ],
            a_send.at[i],
            a_recv.at[i],
            dev_z(i),
        ).wait()
        return carry

    lax.fori_loop(1, NZ, wait_a, 0)
    got = recv_a[...].astype(f32)
    mine = got[:, 0:16, :].reshape(8, 2, 8, DH)
    own = jnp.concatenate([mine[:, 0].reshape(64, DH), mine[:, 1].reshape(64, DH)], axis=0)
    own_w = jnp.sum(got[:, 16:32, :], axis=0)
    slots[pl.ds(chip, 1), 0:BLOCK, :] = own.astype(bf16)[None]
    slots[pl.ds(chip, 1), BLOCK : BLOCK + 16, :] = own_w.astype(bf16)[None]

    def near_first(n):
        return n + (n // 2) * (1 - 2 * (n % 2))

    def start_g(m, carry):
        dx = near_first(m // NY)
        dy = near_first(m % NY)
        i = dx * NY + dy
        copy_of(
            slots.at[chip], slots.at[chip], g_send.at[i], g_recv.at[i], dev_chip(dx, dy)
        ).start()
        return carry

    lax.fori_loop(1, CHIPS, start_g, 0)

    def row_of(shape, of_core):
        r = iota(shape, 0)
        slot = (r // 8) * 4 + r % 4
        return 16 * (slot * 2 + of_core) + 2 * z + (r // 4) % 2

    here = row_of((ROWS, 512), core) == iota((ROWS, 512), 1)
    there = row_of((ROWS, 512), 1 - core) == iota((ROWS, 512), 1)
    rw_col = jnp.sum(jnp.where(here, row_weight[...], 0.0), axis=1, keepdims=True)
    row_scale[...] = jnp.broadcast_to(rw_col * loss_scale, (ROWS, 128))
    load_logits.wait()
    pick = jnp.where(there, 1.0, 0.0).astype(bf16)
    sib_logits[...] = jnp.dot(pick, logits[...], preferred_element_type=f32).astype(bf16)
    share_logits = copy_of(
        sib_logits, own_logits.at[core], k_send.at[1], k_recv.at[1], sibling
    )
    share_logits.start()
    pick = jnp.where(here, 1.0, 0.0).astype(bf16)
    own_logits[pl.ds(core, 1)] = jnp.dot(
        pick, logits[...], preferred_element_type=f32
    ).astype(bf16)[None]
    share_keys.wait()
    transpose_keys(1 - core)
    limit = offset[0] - chip * BOTH

    def is_allowed():
        return iota((ROWS, BOTH), 1) <= limit + row_of((ROWS, 1), core)

    share_logits.wait()
    tlogits = jnp.concatenate([own_logits[0], own_logits[1]], axis=1).astype(f32)
    tmasked = jnp.where(is_allowed(), tlogits, masked_value)
    tpeak = jnp.max(tmasked, axis=1, keepdims=True)
    texp = jnp.where(is_allowed(), jnp.exp(tmasked - tpeak), 0.0)
    target[...] = texp
    ttotal = jnp.sum(texp, axis=1, keepdims=True)

    def forward(m, carry):
        dx = near_first(m)
        gi = (x + NX - dx) % NX

        def arrive(dy, c2):
            i = dx * NY + dy

            @pl.when(i > 0)
            def _():
                copy_of(
                    slots.at[chip],
                    slots.at[chip_at(NX - dx, NY - dy)],
                    g_send.at[i],
                    g_recv.at[i],
                    dev_chip(dx, dy),
                ).wait()

            return c2

        lax.fori_loop(0, NY, arrive, 0)
        block = slots[pl.ds(gi * GROUP, GROUP)]
        q = block[:, 0:BLOCK, :].reshape(GROUP * BLOCK, DH)
        w_tiles = []
        for i in range(GROUP):
            w_row = block[i, BLOCK : BLOCK + 16, :].astype(f32)[0:1] * head_scale
            w_col = jnp.broadcast_to(w_row, (128, 128)).T
            w_tiles.append(w_col.reshape(2, 8, 8, 128))
            qw = block[i, 0:BLOCK, :].astype(f32) * w_col
            query_w[:, pl.ds(pl.multiple_of((gi * GROUP + i) * 128, 128), 128)] = qw.T.astype(bf16)
        for c in range(NCHUNK):
            at = slice(c * CHUNK, (c + 1) * CHUNK)
            dotted = jnp.dot(q, keys_t[:, at], preferred_element_type=f32)
            active = jnp.maximum(dotted, 0.0)
            relu[pl.ds(gi * GROUP, GROUP), :, at] = active.reshape(GROUP, BLOCK, CHUNK).astype(bf16)
            active = active.reshape(GROUP, 2, 8, 8, CHUNK)
            for l in range(CHUNK // 128):
                tiles = []
                for j in range(2):
                    for i in range(GROUP):
                        part = active[i, j, :, :, l * 128 : l * 128 + 128] * w_tiles[i][j]
                        tiles.append(jnp.sum(part, axis=0))
                score[
                    pl.ds(pl.multiple_of(gi * 8, 8), 8),
                    c * CHUNK + l * 128 : c * CHUNK + l * 128 + 128,
                ] = fold_rows(tiles)
        return carry

    lax.fori_loop(0, NX, forward, 0)

    masked = jnp.where(is_allowed(), score[...], masked_value)
    peak = jnp.max(masked, axis=1, keepdims=True)
    exps = jnp.where(is_allowed(), jnp.exp(masked - peak), 0.0)
    score[...] = exps
    total = jnp.sum(exps, axis=1, keepdims=True)
    lane = iota((ROWS, 128), 1)
    stats = jnp.where(
        lane == 0,
        peak,
        jnp.where(lane == 1, total, jnp.where(lane == 2, tpeak, jnp.where(lane == 3, ttotal, 0.0))),
    )
    local = jnp.concatenate([stats, jnp.zeros((128 - ROWS, 128), f32)], axis=0).T[0:8]
    stat_in[0] = local

    def stat_copy(i):
        return copy_of(
            stat_in.at[0], stat_in.at[i], st_send.at[i], st_recv.at[i], dev_chip(i // NY, i % NY)
        )

    def start_stat(m, carry):
        stat_copy((m + 9) % (CHIPS - 1) + 1).start()
        return carry

    lax.fori_loop(0, CHIPS - 1, start_stat, 0)

    def wait_stat(i, carry):
        stat_copy(i).wait()
        return carry

    lax.fori_loop(1, CHIPS, wait_stat, 0)
    every = [stat_in[i] for i in range(CHIPS)]
    top = functools.reduce(jnp.maximum, every)
    total = sum(s * pltpu.roll(jnp.exp(s - top), 1, 0) for s in every)
    total = jnp.where(iota((8, 128), 0) < 4, total, 1.0)
    shares = jnp.exp(local - top) / pltpu.roll(total, 7, 0)
    shares = jnp.concatenate([shares, jnp.zeros((120, 128), f32)], axis=0).T[0:ROWS]
    prob_scale = shares[:, 0:1] * row_scale[:, 0:1]
    target_scale = shares[:, 2:3] * row_scale[:, 0:1]
    score[...] = score[...] * prob_scale - target[...] * target_scale

    def key_chunk(of_core, dz):
        first = of_core * KEYS + ((z + dz) % NZ) * CHUNK
        at = pl.ds(pl.multiple_of(first, CHUNK), CHUNK)
        act = relu[:, :, at].reshape(CHIPS, 2, 4, 16, CHUNK)
        tile = score[:, at]
        rows = jnp.concatenate(
            [
                jnp.broadcast_to(tile[i * 8 + j * 4 + k : i * 8 + j * 4 + k + 1], (16, CHUNK))
                for i in range(NX)
                for k in range(GROUP)
                for j in range(2)
            ],
            axis=0,
        )
        rows = rows.astype(bf16).reshape(CHIPS, 2, 1, 16, CHUNK)
        pre = jnp.where(act > 0, rows, jnp.zeros_like(rows)).reshape(CHIPS * BLOCK, CHUNK)
        return jnp.dot(query_w[...], pre, preferred_element_type=f32)

    def sib_copy(n):
        return copy_of(
            key_sib_out.at[n], key_sib_in.at[n], sib_send.at[n], sib_recv.at[n], sibling
        )

    def key_copy(n):
        return copy_of(
            key_out.at[n], key_in.at[n], key_send.at[n], key_recv.at[n], dev_z(far_first(n))
        )

    def key_pass_on(n):
        sib_copy(n).wait()
        key_out[n] = (key_own[n] + key_sib_in[n].astype(f32)).astype(bf16)
        key_copy(n).start()

    def key_product(n):
        theirs = key_chunk(1 - core, far_first(n))
        ours = key_chunk(core, far_first(n))
        key_sib_out[n] = theirs.astype(bf16)
        sib_copy(n).start()
        key_own[n] = ours

    def key_step(n, carry):
        key_product(n)

        @pl.when(n >= EARLY + LAG)
        def _():
            key_pass_on(n - LAG)

        return carry

    lax.fori_loop(0, EARLY, key_step, 0)

    def backward_query(gi):
        acc = jnp.zeros((GROUP * BLOCK, DH), f32)
        for c in range(NCHUNK):
            at = slice(c * CHUNK, (c + 1) * CHUNK)
            act = relu[pl.ds(gi * GROUP, GROUP), :, at].reshape(GROUP, 2, 4, 16, CHUNK)
            tile = score[pl.ds(pl.multiple_of(gi * 8, 8), 8), at]
            rows = jnp.concatenate(
                [
                    jnp.broadcast_to(tile[j * 4 + k : j * 4 + k + 1], (16, CHUNK))
                    for k in range(GROUP)
                    for j in range(2)
                ],
                axis=0,
            )
            rows = rows.astype(bf16).reshape(GROUP, 2, 1, 16, CHUNK)
            pre = jnp.where(act > 0, rows, jnp.zeros_like(rows)).reshape(GROUP * BLOCK, CHUNK)
            acc = acc + jnp.dot(pre, keys[at, :], preferred_element_type=f32)
        return acc.reshape(GROUP, BLOCK, DH)

    def sum_copy(dx, dy):
        i = dx * NY + dy
        return copy_of(
            sum_out.at[chip_at(dx, dy)],
            sum_in.at[i],
            sum_send.at[i],
            sum_recv.at[i],
            dev_chip(dx, dy),
        )

    def backward(n, carry):
        dx = 2 - n + (n // 2) * (3 - 2 * (n % 2))
        g = (x + dx) % NX
        sum_out[pl.ds(g * GROUP, GROUP)] = backward_query(g).astype(bf16)

        def to_chip(dy, c2):
            @pl.when(dx * NY + dy > 0)
            def _():
                sum_copy(dx, dy).start()

            return c2

        lax.fori_loop(0, NY, to_chip, 0)

        @pl.when(n == WHEN)
        def _():
            for k in range(EARLY):
                key_pass_on(k)

        return carry

    lax.fori_loop(0, NX, backward, 0)
    lax.fori_loop(EARLY, NZ - 1, key_step, 0)

    def wait_sum(m, acc):
        n = m // NY
        i = (2 - n + (n // 2) * (3 - 2 * (n % 2))) * NY + NY - 1 - m % NY
        sum_copy(i // NY, i % NY).wait()
        return acc + sum_in[i].astype(f32)

    total_g = lax.fori_loop(0, CHIPS - 1, wait_sum, sum_out[chip].astype(f32))
    total_g = total_g.reshape(2, 8, 8, DH)
    for h in range(NZ):
        back_out[h, 0:8, :] = total_g[0, h]
        back_out[h, 8:16, :] = total_g[1, h]

    def start_back(n, carry):
        i = far_first(n)
        copy_of(
            back_out.at[(z + i) % NZ], back_in.at[z], back_send.at[i], back_recv.at[i], dev_z(i)
        ).start()
        return carry

    lax.fori_loop(0, NZ - 1, start_back, 0)
    back_in[pl.ds(z, 1)] = back_out[pl.ds(z, 1)]

    for k in range(max(NZ - 1 - LAG, EARLY), NZ - 1):
        key_pass_on(k)
    key_product(NZ - 1)
    sib_copy(NZ - 1).wait()

    def wait_key(n, acc):
        key_copy(n).wait()
        return acc + key_in[n].astype(f32)

    acc = key_own[NZ - 1] + key_sib_in[NZ - 1].astype(f32)
    key_sum[...] = lax.fori_loop(0, NZ - 1, wait_key, acc).T

    def wait_back(i, carry):
        copy_of(
            back_out.at[(z + i) % NZ],
            back_in.at[(z + NZ - i) % NZ],
            back_send.at[i],
            back_recv.at[i],
            dev_z(i),
        ).wait()
        return carry

    lax.fori_loop(1, NZ, wait_back, 0)
    back[...] = back_in[...].reshape(128, DH)


def finish(back, key_sum, query, weights, query_grad, key_grad, weight_grad):
    head_scale = DH**-0.5
    key_grad[...] = key_sum[...]
    grad = back[...] * head_scale
    spread = jnp.where(iota((16, 128), 0) == iota((16, 128), 1) // 8, 1.0, 0.0)
    w_rows = lax.dot_general(
        spread,
        weights[...].astype(f32),
        (((0,), (1,)), ((), ())),
        preferred_element_type=f32,
    )
    w_rows = jnp.where(iota((128, 8), 0) % 8 == iota((128, 8), 1), w_rows, 0.0)
    query_grad[...] = grad * jnp.sum(w_rows, axis=1, keepdims=True)
    w_grad = jnp.sum(grad * query[...].astype(f32), axis=1, keepdims=True).reshape(16, 8, 1)
    out = jnp.zeros((8, 128), f32)
    for t in range(16):
        out = jnp.where(iota((8, 128), 1) == t, w_grad[t], out)
    weight_grad[...] = out[:, 0:16]


def per_device(query, weights, keys, main_logits, row_weight, offset):
    vmem = pl.BlockSpec(memory_space=pltpu.VMEM)
    anywhere = pl.BlockSpec(memory_space=pl.ANY)
    dma = pltpu.SemaphoreType.DMA
    query = query.reshape(128, DH)
    weights = weights.T
    back, key_sum = pl.pallas_call(
        kernel,
        out_shape=[
            jax.ShapeDtypeStruct((128, DH), f32),
            jax.ShapeDtypeStruct((CHUNK, DH), f32),
        ],
        in_specs=[
            anywhere,
            anywhere,
            anywhere,
            anywhere,
            vmem,
            pl.BlockSpec(memory_space=pltpu.SMEM),
        ],
        out_specs=[vmem, vmem],
        scratch_shapes=[
            pltpu.VMEM((128, DH), bf16),
            pltpu.VMEM((8, 16), bf16),
            pltpu.VMEM((BOTH, DH), bf16),
            pltpu.VMEM((DH, BOTH), bf16),
            pltpu.VMEM((512, KEYS), bf16),
            pltpu.VMEM((2, ROWS, KEYS), bf16),
            pltpu.VMEM((ROWS, KEYS), bf16),
            pltpu.VMEM((NZ, 32, 128), bf16),
            pltpu.VMEM((NZ, 32, 128), bf16),
            pltpu.VMEM((CHIPS, BLOCK + 16, DH), bf16),
            pltpu.VMEM((CHIPS, BLOCK, BOTH), bf16),
            pltpu.VMEM((ROWS, BOTH), f32),
            pltpu.VMEM((ROWS, BOTH), f32),
            pltpu.VMEM((DH, CHIPS * BLOCK), bf16),
            pltpu.VMEM((ROWS, 128), f32),
            pltpu.VMEM((CHIPS, 8, 128), f32),
            pltpu.VMEM((CHIPS, BLOCK, DH), bf16),
            pltpu.VMEM((CHIPS, BLOCK, DH), bf16),
            pltpu.VMEM((NZ, DH, CHUNK), f32),
            pltpu.VMEM((NZ, DH, CHUNK), bf16),
            pltpu.VMEM((NZ, DH, CHUNK), bf16),
            pltpu.VMEM((NZ, DH, CHUNK), bf16),
            pltpu.VMEM((NZ, DH, CHUNK), bf16),
            pltpu.VMEM((NZ, 16, DH), f32),
            pltpu.VMEM((NZ, 16, DH), f32),
            dma((4,)),
            dma((NZ,)),
            dma((NZ,)),
            dma((2,)),
            dma((2,)),
            dma((CHIPS,)),
            dma((CHIPS,)),
            dma((CHIPS,)),
            dma((CHIPS,)),
            dma((CHIPS,)),
            dma((CHIPS,)),
            dma((NZ,)),
            dma((NZ,)),
            dma((NZ,)),
            dma((NZ,)),
            dma((NZ,)),
            dma((NZ,)),
        ],
        compiler_params=pltpu.CompilerParams(
            collective_id=0, has_side_effects=True, vmem_limit_bytes=56 * 2**20
        ),
    )(
        query,
        weights,
        keys,
        main_logits,
        row_weight.reshape(1, 512),
        offset,
    )
    query_grad, key_grad, weight_grad = pl.pallas_call(
        finish,
        out_shape=[
            jax.ShapeDtypeStruct((128, DH), f32),
            jax.ShapeDtypeStruct((CHUNK, DH), f32),
            jax.ShapeDtypeStruct((8, 16), f32),
        ],
        in_specs=[vmem] * 4,
        out_specs=[vmem] * 3,
    )(back, key_sum, query, weights)
    return query_grad.reshape(16, 8, DH), key_grad, weight_grad.T


def solution(mesh):
    in_specs = (P("ctx", "head", None), P("ctx", "head"), P("ctx", None), P(None, "ctx"), P(), P())
    out_specs = (P("ctx", "head", None), P(("ctx", "head"), None), P("ctx", "head"))
    return jax.shard_map(
        per_device, mesh=mesh, in_specs=in_specs, out_specs=out_specs, check_vma=False
    )
```
